128 devices in a mesh: section: 4 (over x), dp: 32 (over z, y, core).
Axes of the slice: x: 4, y: 4, z: 4, core: 2. Of those that a mesh axis runs over, the one named last changes fastest.
Arguments:
- tokens: bfloat16 [4096, 8192], P('dp'), may hold values from -6 to 6
- blocks_in: bfloat16 [4, 160, 128, 128], P('section', 'dp'), may hold values from -0.078125 to 0.078125
- blocks_out: bfloat16 [4, 160, 128, 128], P('section', 'dp'), may hold values from -0.3125 to 0.3125
- pos_in: int32 [4, 160], P('section', 'dp'), may hold values from 0 to 256, as said below
- pos_out: int32 [4, 160], P('section', 'dp'), may hold values from 0 to 256, as said below
- cotangent: bfloat16 [4096, 8192], P('dp'), may hold values from -0.08984375 to 0.08984375
Outputs:
- grad_in: bfloat16 [4, 160, 128, 128], P('section', 'dp')
- grad_out: bfloat16 [4, 160, 128, 128], P('section', 'dp')
The draws below stay inside these ranges and needn't reach their ends.
Inputs may be any that keep to these rules, and one draw needn't show every extreme that they name: For each layer the first k slots (k from 110 to 160) hold distinct block numbers and the other slots hold 256, marking an empty slot; in each of pos_in and pos_out some layer fills all 160 slots. `pos_out`: as for pos_in, drawn independently.
All inputs are finite; a program needn't handle non-finite values.
Results may differ from the reference program's by a relative error of at most 0.023.
Values may be sent and summed in bfloat16 or wider, within the bound.
No kernel may reach another device: no remote copies, remote signals or barrier semaphores. Data moves between devices by JAX's collectives and lax.ppermute only.
A program may use at most 128 MiB of HBM per device.

```python
import jax
import jax.numpy as jnp
from jax import lax

D = 8192
RANK = 512
BLOCK = 128
CAP = 160
LIVE_LO = 110
NBLK = 256
TOK_DEV = 128
LAYERS = 4
TOKENS = 4096
N_DP = 32


def block_places(key, which):
    base = jax.random.fold_in(key, 77)
    count_key = jax.random.fold_in(jax.random.fold_in(base, 1), which)
    full_key = jax.random.fold_in(jax.random.fold_in(base, 2), which)
    perm_key = jax.random.fold_in(jax.random.fold_in(base, 3), which)
    counts = jax.random.randint(count_key, (LAYERS,), LIVE_LO, CAP + 1)
    filled = jax.random.randint(full_key, (), 0, LAYERS)
    counts = jnp.where(jnp.arange(LAYERS) == filled, CAP, counts)
    layer_keys = jax.random.split(perm_key, LAYERS)
    perms = jax.vmap(lambda kk: jax.random.permutation(kk, NBLK)[:CAP])(layer_keys)
    slots = jnp.arange(CAP)
    return jnp.where(slots[None, :] < counts[:, None], perms, NBLK).astype(jnp.int32)


def draw_pos_in(key, part):
    return block_places(key, 0)


def draw_pos_out(key, part):
    return block_places(key, 1)


def block_levels(stream_key, dims, cuts, least, largest):
    gain = 1.0
    for dim, blocks in cuts:
        heights = jax.random.uniform(jax.random.fold_in(jax.random.fold_in(stream_key, 6), dim), (blocks,), jnp.float32, least / len(cuts), largest / len(cuts))
        gain = gain * jnp.repeat(jnp.exp(heights), dims[dim] // blocks).reshape((-1,) + (1,) * (len(dims) - 1 - dim))
    return gain


def centred(own_key, shape, deviation, limit, pieces=(), kind=jnp.bfloat16):
    values = deviation * jax.random.normal(own_key, shape, jnp.float32)
    if pieces:
        values = values * block_levels(own_key, shape, pieces, -0.22, 0.18)
    return jnp.clip(values, -limit, limit).astype(kind)


def setup_inputs(seed: int = 0) -> dict:
    key_list = jax.random.split(jax.random.key(seed), 7)
    return {
        "tokens": centred(key_list[0], (TOKENS, D), 1.0, 6.0, ((0, 32),)),
        "blocks_in": centred(key_list[1], (LAYERS, CAP, BLOCK, BLOCK), (CAP * BLOCK * BLOCK // RANK) ** -0.5, 0.078125, ((0, 4), (1, 32))),
        "blocks_out": centred(key_list[2], (LAYERS, CAP, BLOCK, BLOCK), (CAP * BLOCK * BLOCK // D) ** -0.5, 0.3125, ((0, 4), (1, 32))),
        "pos_in": draw_pos_in(jax.random.fold_in(key_list[6], 71), 0),
        "pos_out": draw_pos_out(jax.random.fold_in(key_list[6], 71), 0),
        "cotangent": centred(key_list[5], (TOKENS, D), 0.015625, 0.08984375, ((0, 32),)),
    }


EPS = 1e-05

def expand(blocks, places, rows_b, cols_b):
    flat = jnp.zeros((rows_b * cols_b, BLOCK, BLOCK), blocks.dtype)
    flat = flat.at[places].set(blocks, mode='drop')
    return flat.reshape(rows_b, cols_b, BLOCK, BLOCK).transpose(0, 2, 1, 3).reshape(rows_b * BLOCK, cols_b * BLOCK)

def pack(dense, places, rows_b, cols_b):
    blocks = dense.reshape(rows_b, BLOCK, cols_b, BLOCK).transpose(0, 2, 1, 3).reshape(rows_b * cols_b, BLOCK, BLOCK)
    return jnp.take(blocks, places, axis=0, mode='fill', fill_value=0.0)

def norm_parts(hidden):
    wide = hidden.astype(jnp.float32)
    scale = jnp.sqrt(lax.optimization_barrier(jnp.mean(wide * wide, axis=-1, keepdims=True)) + EPS)
    return (wide, scale)

def device_sums(left, right, places, rows_b, cols_b):
    left_dev = left.reshape(N_DP, TOK_DEV, left.shape[1])
    right_dev = right.reshape(N_DP, TOK_DEV, right.shape[1])

    def step(total, pair):
        part = lax.dot_general(pair[0], pair[1], (((0,), (0,)), ((), ())), preferred_element_type=jnp.float32)
        packed = pack(part, places, rows_b, cols_b).astype(jnp.bfloat16)
        packed = lax.optimization_barrier(packed)
        return (total + packed.astype(jnp.float32), None)
    init = jnp.zeros((places.shape[0], BLOCK, BLOCK), jnp.float32)
    total, _ = lax.scan(step, init, (left_dev, right_dev))
    return total

def reference(tokens, blocks_in, blocks_out, pos_in, pos_out, cotangent):
    rows_d = D // BLOCK
    rows_k = RANK // BLOCK
    mats_a = [expand(blocks_in[l], pos_in[l], rows_d, rows_k) for l in range(LAYERS)]
    mats_b = [expand(blocks_out[l], pos_out[l], rows_k, rows_d) for l in range(LAYERS)]
    states = [tokens]
    for l in range(LAYERS):
        wide, scale = norm_parts(states[l])
        normed = (wide / scale).astype(jnp.bfloat16)
        pre = jnp.dot(normed, mats_a[l], preferred_element_type=jnp.float32)
        act = (pre * jax.nn.sigmoid(pre)).astype(jnp.bfloat16)
        states.append((wide + jnp.dot(act, mats_b[l], preferred_element_type=jnp.float32)).astype(jnp.bfloat16))
    upstream = cotangent
    grads_in = [None] * LAYERS
    grads_out = [None] * LAYERS
    for l in reversed(range(LAYERS)):
        wide, scale = norm_parts(states[l])
        unit = wide / scale
        normed = unit.astype(jnp.bfloat16)
        pre = jnp.dot(normed, mats_a[l], preferred_element_type=jnp.float32)
        sig = jax.nn.sigmoid(pre)
        act = (pre * sig).astype(jnp.bfloat16)
        dact = lax.dot_general(upstream, mats_b[l], (((1,), (1,)), ((), ())), preferred_element_type=jnp.float32)
        dpre = (dact * sig * (1.0 + pre * (1.0 - sig))).astype(jnp.bfloat16)
        dnorm = lax.dot_general(dpre, mats_a[l], (((1,), (1,)), ((), ())), preferred_element_type=jnp.float32)
        grads_in[l] = device_sums(normed, dpre, pos_in[l], rows_d, rows_k).astype(jnp.bfloat16)
        grads_out[l] = device_sums(act, upstream, pos_out[l], rows_k, rows_d).astype(jnp.bfloat16)
        inner = lax.optimization_barrier(jnp.mean(dnorm * unit, axis=-1, keepdims=True))
        upstream = (upstream.astype(jnp.float32) + (dnorm - unit * inner) / scale).astype(jnp.bfloat16)
    return (jnp.stack(grads_in), jnp.stack(grads_out))
```

```python
import functools

import jax
import jax.numpy as jnp
from jax import lax
from jax.experimental import pallas as pl
from jax.experimental.pallas import tpu as pltpu
from jax.sharding import PartitionSpec as P

D = 8192
RANK = 512
BLOCK = 128
ROWS_D = D // BLOCK
ROWS_K = RANK // BLOCK
NBLK = ROWS_D * ROWS_K
EPS = 1e-05
CHUNK = 1024
BLOCKS = CHUNK // BLOCK
NT = (((1,), (1,)), ((), ()))
NN = (((1,), (0,)), ((), ()))
TN = (((0,), (0,)), ((), ()))
PAIR = [(0, 1), (1, 0), (2, 3), (3, 2)]
UP = [(0, 3), (1, 2)]
DOWN = [(3, 0), (2, 1)]


def dot(left, right, dims):
    return lax.dot_general(left, right, dims, preferred_element_type=jnp.float32)


def fetch(where_ref, weights_ref, base, number):
    code = where_ref[base + number]
    safe = jnp.maximum(code, 0)
    block = weights_ref[safe >> 3, 0, 0, safe & 7]
    return lax.select(code >= 0, block, jnp.zeros_like(block))


def assemble_in(where_ref, weights_ref, dense_ref, base, chunk):
    for row in range(BLOCKS):
        for col in range(ROWS_K):
            dense_ref[row * BLOCK : (row + 1) * BLOCK, col * BLOCK : (col + 1) * BLOCK] = fetch(
                where_ref, weights_ref, base, (chunk * BLOCKS + row) * ROWS_K + col
            )


def assemble_out(where_ref, weights_ref, dense_ref, base, chunk):
    for row in range(ROWS_K):
        for col in range(BLOCKS):
            dense_ref[row * BLOCK : (row + 1) * BLOCK, col * BLOCK : (col + 1) * BLOCK] = fetch(
                where_ref, weights_ref, base, row * ROWS_D + chunk * BLOCKS + col
            )


def columns(chunk):
    return pl.ds(pl.multiple_of(chunk * CHUNK, CHUNK), CHUNK)


def root(hidden_ref):
    def step(chunk, total):
        wide = hidden_ref[:, columns(chunk)].astype(jnp.float32)
        return total + jnp.sum(wide * wide, axis=-1, keepdims=True)

    total = lax.fori_loop(0, D // CHUNK, step, jnp.zeros((hidden_ref.shape[0], 1), jnp.float32))
    return jnp.sqrt(total / D + EPS)


def forward_kernel(swap_ref, where_ref, first_ref, weights_ref, second_ref, last_ref, pre_ref, act_ref, scale_ref, dense_in, dense_out):
    step = pl.program_id(0)

    def down(layer, hidden_ref):
        base = ((layer ^ swap_ref[0]) * 2) * NBLK
        scale = root(hidden_ref)
        scale_ref[layer] = jnp.broadcast_to(scale, scale_ref.shape[1:])
        pre_ref[layer] = jnp.zeros(pre_ref.shape[1:], jnp.float32)

        @pl.loop(0, D // CHUNK)
        def _(chunk):
            assemble_in(where_ref, weights_ref, dense_in, base, chunk)
            normed = (hidden_ref[:, columns(chunk)].astype(jnp.float32) / scale).astype(jnp.bfloat16)
            pre_ref[layer] += dot(normed, dense_in[...], NN)

    def up(layer, hidden_ref, next_ref):
        base = ((layer ^ swap_ref[0]) * 2 + 1) * NBLK
        pre = pre_ref[layer]
        act = (pre * jax.nn.sigmoid(pre)).astype(jnp.bfloat16)
        act_ref[layer] = act

        @pl.loop(0, D // CHUNK)
        def _(chunk):
            assemble_out(where_ref, weights_ref, dense_out, base, chunk)
            moved = dot(act_ref[layer], dense_out[...], NN)
            next_ref[:, columns(chunk)] = (hidden_ref[:, columns(chunk)].astype(jnp.float32) + moved).astype(jnp.bfloat16)

    pl.when(step == 0)(lambda: down(0, first_ref))
    pl.when(step == 1)(lambda: up(0, first_ref, second_ref))
    pl.when(step == 2)(lambda: down(1, second_ref))
    pl.when(step == 3)(lambda: up(1, second_ref, last_ref))


def backward_kernel(
    swap_ref, where_ref, first_ref, second_ref, grad_ref, pre_ref, scale_ref, weights_ref, middle_ref, earlier_ref, dpre_ref, total, inner, dense_in, dense_out
):
    step = pl.program_id(0)

    def up(layer, upstream_ref):
        base = ((layer ^ swap_ref[0]) * 2 + 1) * NBLK
        total[...] = jnp.zeros(total.shape, jnp.float32)

        @pl.loop(0, D // CHUNK)
        def _(chunk):
            assemble_out(where_ref, weights_ref, dense_out, base, chunk)
            total[...] += dot(upstream_ref[:, columns(chunk)], dense_out[...], NT)

        pre = pre_ref[layer]
        sig = jax.nn.sigmoid(pre)
        dpre = (total[...] * sig * (1.0 + pre * (1.0 - sig))).astype(jnp.bfloat16)
        dpre_ref[layer] = dpre
        mean = jnp.sum(dpre.astype(jnp.float32) * pre, axis=-1, keepdims=True) / D
        inner[...] = jnp.broadcast_to(mean, inner.shape)

    def down(layer, hidden_ref, upstream_ref, out_ref):
        base = ((layer ^ swap_ref[0]) * 2) * NBLK
        scale = scale_ref[layer][:, :1]
        mean = inner[:, :1]

        @pl.loop(0, D // CHUNK)
        def _(chunk):
            assemble_in(where_ref, weights_ref, dense_in, base, chunk)
            dnorm = dot(dpre_ref[layer], dense_in[...], NT)
            unit = hidden_ref[:, columns(chunk)].astype(jnp.float32) / scale
            out_ref[:, columns(chunk)] = (
                upstream_ref[:, columns(chunk)].astype(jnp.float32) + (dnorm - unit * mean) / scale
            ).astype(jnp.bfloat16)

    pl.when(step == 0)(lambda: up(1, grad_ref))
    pl.when(step == 1)(lambda: down(1, second_ref, grad_ref, middle_ref))
    pl.when(step == 2)(lambda: up(0, middle_ref))
    pl.when(step == 3)(lambda: down(0, first_ref, middle_ref, earlier_ref))


def gradient_kernel(
    swap_ref, places_ref, first_ref, second_ref, grad_ref, middle_ref, dpre_ref, act_ref, scale_ref, out_ref, dense, turned
):
    step = pl.program_id(0)
    owners, slots = out_ref.shape[0], out_ref.shape[3]
    dense[NBLK] = jnp.zeros((BLOCK, BLOCK), jnp.bfloat16)

    def pick(base):
        @pl.loop(0, owners)
        def _(owner):
            for slot in range(slots):
                out_ref[owner, 0, 0, slot] = dense[places_ref[base + owner * slots + slot]]

    def down(layer, hidden_ref):
        scale = scale_ref[layer][:, :1]

        @pl.loop(0, ROWS_D)
        def _(row):
            block = pl.ds(pl.multiple_of(row * BLOCK, BLOCK), BLOCK)
            normed = (hidden_ref[:, block].astype(jnp.float32) / scale).astype(jnp.bfloat16)
            part = dot(normed, dpre_ref[layer], TN).astype(jnp.bfloat16)
            for col in range(ROWS_K):
                dense[row * ROWS_K + col] = part[:, col * BLOCK : (col + 1) * BLOCK]

        pick(((layer ^ swap_ref[0]) * 2) * owners * slots)

    def up(layer, upstream_ref):
        turned[...] = act_ref[layer].astype(jnp.float32).T.astype(jnp.bfloat16)

        @pl.loop(0, ROWS_D // 2)
        def _(pair):
            block = pl.ds(pl.multiple_of(pair * 2 * BLOCK, 2 * BLOCK), 2 * BLOCK)
            part = dot(turned[...], upstream_ref[:, block], NN).astype(jnp.bfloat16)
            for row in range(ROWS_K):
                for col in range(2):
                    dense[row * ROWS_D + pair * 2 + col] = part[
                        row * BLOCK : (row + 1) * BLOCK, col * BLOCK : (col + 1) * BLOCK
                    ]

        pick(((layer ^ swap_ref[0]) * 2 + 1) * owners * slots)

    pl.when(step == 0)(lambda: up(1, grad_ref))
    pl.when(step == 1)(lambda: down(1, second_ref))
    pl.when(step == 2)(lambda: up(0, middle_ref))
    pl.when(step == 3)(lambda: down(0, first_ref))


def whole(*shape):
    return pl.BlockSpec(shape, lambda step, *_: (0,) * len(shape))


def params(flops, moved):
    return dict(
        compiler_params=pltpu.CompilerParams(
            dimension_semantics=("arbitrary",), vmem_limit_bytes=56 * 1024 * 1024
        ),
        cost_estimate=pl.CostEstimate(flops=flops, bytes_accessed=moved, transcendentals=0),
    )


def per_device(tokens, blocks_in, blocks_out, pos_in, pos_out, cotangent):
    here = lax.axis_index("section")
    owners = lax.axis_size("dp")
    slots = blocks_in.shape[1]
    rows = tokens.shape[0] // 2
    swap = (here % 2).astype(jnp.int32).reshape(1)
    upper = here >= 2
    half = jnp.where((here == 1) | (here == 2), rows, 0)

    own = jnp.stack([blocks_in[0], blocks_out[0]])
    both = jnp.stack([own, lax.ppermute(own, "section", PAIR)])
    weights = lax.all_gather(both, "dp", axis=0)
    own_places = jnp.stack([pos_in[0], pos_out[0]])
    both_places = jnp.stack([own_places, lax.ppermute(own_places, "section", PAIR)])
    places = lax.all_gather(both_places, "dp", axis=0).transpose(1, 2, 0, 3)
    codes = jnp.arange(owners, dtype=jnp.int32)[:, None] * 8 + jnp.arange(slots, dtype=jnp.int32)
    named = places[..., None] == jnp.arange(NBLK, dtype=jnp.int32)
    where = jnp.max(jnp.where(named, codes[..., None], -1), axis=(2, 3)).reshape(-1)
    places = places.reshape(-1)

    first_tokens = lax.dynamic_slice_in_dim(tokens, half, rows, 0)
    last_grads = lax.dynamic_slice_in_dim(cotangent, half, rows, 0)

    wide = jax.ShapeDtypeStruct((rows, D), jnp.bfloat16)
    narrow = jax.ShapeDtypeStruct((2, rows, RANK), jnp.bfloat16)
    narrow32 = jax.ShapeDtypeStruct((2, rows, RANK), jnp.float32)
    lane32 = jax.ShapeDtypeStruct((2, rows, BLOCK), jnp.float32)
    piece = (owners, 1, 1, slots, BLOCK, BLOCK)
    moved = weights.size * 2
    dense = [pltpu.VMEM((CHUNK, RANK), jnp.bfloat16), pltpu.VMEM((RANK, CHUNK), jnp.bfloat16)]

    forward = pl.pallas_call(
        forward_kernel,
        out_shape=(wide, wide, narrow32, narrow, lane32),
        grid_spec=pltpu.PrefetchScalarGridSpec(
            num_scalar_prefetch=2,
            grid=(4,),
            in_specs=[
                whole(rows, D),
                pl.BlockSpec(piece, lambda step, swap, _: (0, (step // 2) ^ swap[0], step % 2, 0, 0, 0)),
            ],
            out_specs=[
                whole(rows, D),
                whole(rows, D),
                whole(2, rows, RANK),
                whole(2, rows, RANK),
                whole(2, rows, BLOCK),
            ],
            scratch_shapes=dense,
        ),
        name="forward_layers",
        **params(8 * rows * D * RANK, moved),
    )
    backward = pl.pallas_call(
        backward_kernel,
        out_shape=(wide, wide, narrow),
        grid_spec=pltpu.PrefetchScalarGridSpec(
            num_scalar_prefetch=2,
            grid=(4,),
            in_specs=[
                whole(rows, D),
                whole(rows, D),
                whole(rows, D),
                whole(2, rows, RANK),
                whole(2, rows, BLOCK),
                pl.BlockSpec(
                    piece, lambda step, swap, _: (0, (1 - step // 2) ^ swap[0], 1 - step % 2, 0, 0, 0)
                ),
            ],
            out_specs=[whole(rows, D), whole(rows, D), whole(2, rows, RANK)],
            scratch_shapes=[
                pltpu.VMEM((rows, RANK), jnp.float32),
                pltpu.VMEM((rows, BLOCK), jnp.float32),
            ]
            + dense,
        ),
        name="backward_layers",
        **params(8 * rows * D * RANK, moved),
    )
    gradient = pl.pallas_call(
        gradient_kernel,
        out_shape=jax.ShapeDtypeStruct(weights.shape, jnp.bfloat16),
        grid_spec=pltpu.PrefetchScalarGridSpec(
            num_scalar_prefetch=2,
            grid=(4,),
            in_specs=[
                whole(rows, D),
                whole(rows, D),
                whole(rows, D),
                whole(rows, D),
                whole(2, rows, RANK),
                whole(2, rows, RANK),
                whole(2, rows, BLOCK),
            ],
            out_specs=pl.BlockSpec(
                piece, lambda step, swap, _: (0, (1 - step // 2) ^ swap[0], 1 - step % 2, 0, 0, 0)
            ),
            scratch_shapes=[
                pltpu.VMEM((NBLK + 1, BLOCK, BLOCK), jnp.bfloat16),
                pltpu.VMEM((RANK, rows), jnp.bfloat16),
            ],
        ),
        name="slot_gradients",
        **params(8 * rows * D * RANK, moved),
    )

    _, leaving, _, _, _ = forward(swap, where, first_tokens, weights)
    arrived = lax.ppermute(leaving, "section", UP)
    first = jnp.where(upper, arrived, first_tokens)
    second, _, pre, act, scale = forward(swap, where, first, weights)
    _, leaving, _ = backward(swap, where, first, second, last_grads, pre, scale, weights)
    arrived = lax.ppermute(leaving, "section", DOWN)
    grads = jnp.where(upper, last_grads, arrived)
    middle, _, dpre = backward(swap, where, first, second, grads, pre, scale, weights)
    partial = gradient(swap, places, first, second, grads, middle, dpre, act, scale)
    summed = lax.psum_scatter(partial, "dp", scatter_dimension=0, tiled=False)
    own_sum, other_sum = summed[0], summed[1]
    result = own_sum.astype(jnp.float32) + lax.ppermute(other_sum, "section", PAIR).astype(jnp.float32)
    result = result.astype(jnp.bfloat16)
    return (result[0][None], result[1][None])


def solution(mesh):
    in_specs = (
        P("dp", None),
        P("section", "dp", None, None),
        P("section", "dp", None, None),
        P("section", "dp"),
        P("section", "dp"),
        P("dp", None),
    )
    out_specs = (P("section", "dp", None, None), P("section", "dp", None, None))
    return jax.shard_map(
        per_device, mesh=mesh, in_specs=in_specs, out_specs=out_specs, check_vma=False
    )
```

```python
import functools

import jax
import jax.numpy as jnp
from jax import lax
from jax.experimental import pallas as pl
from jax.experimental.pallas import tpu as pltpu
from jax.sharding import PartitionSpec as P

D = 8192
RANK = 512
BLOCK = 128
ROWS_D = D // BLOCK
ROWS_K = RANK // BLOCK
NBLK = ROWS_D * ROWS_K
EPS = 1e-05
CHUNK = 1024
BLOCKS = CHUNK // BLOCK
SPAN = 512
NT = (((1,), (1,)), ((), ()))
NN = (((1,), (0,)), ((), ()))
TN = (((0,), (0,)), ((), ()))
PAIR = [(0, 1), (1, 0), (2, 3), (3, 2)]
UP = [(0, 3), (1, 2)]
DOWN = [(3, 0), (2, 1)]


def dot(left, right, dims):
    return lax.dot_general(left, right, dims, preferred_element_type=jnp.float32)


def fetch(where_ref, weights_ref, number):
    code = where_ref[number]
    safe = jnp.maximum(code, 0)
    block = weights_ref[safe >> 3, 0, 0, safe & 7]
    return lax.select(code >= 0, block, jnp.zeros_like(block))


def rows_in(where_ref, weights_ref, base, row, count):
    return jnp.concatenate(
        [
            jnp.concatenate(
                [fetch(where_ref, weights_ref, base + (row + i) * ROWS_K + col) for col in range(ROWS_K)], axis=1
            )
            for i in range(count)
        ],
        axis=0,
    )


def columns_out(where_ref, weights_ref, base, col, count):
    return jnp.concatenate(
        [
            jnp.concatenate(
                [fetch(where_ref, weights_ref, base + row * ROWS_D + col + i) for i in range(count)], axis=1
            )
            for row in range(ROWS_K)
        ],
        axis=0,
    )


def columns(chunk, width=CHUNK):
    return pl.ds(pl.multiple_of(chunk * width, width), width)


def root(hidden_ref):
    def step(chunk, total):
        wide = hidden_ref[:, columns(chunk)].astype(jnp.float32)
        return total + jnp.sum(wide * wide, axis=-1, keepdims=True)

    total = lax.fori_loop(0, D // CHUNK, step, jnp.zeros((hidden_ref.shape[0], 1), jnp.float32))
    return jnp.sqrt(total / D + EPS)


def forward_kernel(
    swap_ref, where_ref, first_ref, weights_ref, second_ref, last_ref, pre_ref, scale_ref, normed_ref, act_ref
):
    step = pl.program_id(0)

    def down(layer, hidden_ref):
        place = layer ^ swap_ref[0]
        base = place * 2 * NBLK
        scale = root(hidden_ref)
        scale_ref[layer] = jnp.broadcast_to(scale, scale_ref.shape[1:])
        pre_ref[layer] = jnp.zeros(pre_ref.shape[1:], jnp.float32)

        @pl.loop(0, D // CHUNK)
        def _(chunk):
            normed = (hidden_ref[:, columns(chunk)].astype(jnp.float32) / scale).astype(jnp.bfloat16)
            normed_ref[place, :, columns(chunk)] = normed
            dense = rows_in(where_ref, weights_ref, base, chunk * BLOCKS, BLOCKS)
            pre_ref[layer] += dot(normed, dense, NN)

    def up(layer, hidden_ref, next_ref):
        place = layer ^ swap_ref[0]
        base = (place * 2 + 1) * NBLK
        pre = pre_ref[layer]
        act_ref[place] = (pre * jax.nn.sigmoid(pre)).astype(jnp.bfloat16)

        @pl.loop(0, D // CHUNK)
        def _(chunk):
            dense = columns_out(where_ref, weights_ref, base, chunk * BLOCKS, BLOCKS)
            moved = dot(act_ref[place], dense, NN)
            next_ref[:, columns(chunk)] = (hidden_ref[:, columns(chunk)].astype(jnp.float32) + moved).astype(jnp.bfloat16)

    pl.when(step == 0)(lambda: down(0, first_ref))
    pl.when(step == 1)(lambda: up(0, first_ref, second_ref))
    pl.when(step == 2)(lambda: down(1, second_ref))
    pl.when(step == 3)(lambda: up(1, second_ref, last_ref))


def backward_kernel(
    layer, swap_ref, where_ref, hidden_ref, upstream_ref, pre_ref, scale_ref, weights_ref, earlier_ref, dpre_ref, total, inner
):
    step = pl.program_id(0)
    place = layer ^ swap_ref[0]

    @pl.when(step == 0)
    def _():
        base = (place * 2 + 1) * NBLK
        total[...] = jnp.zeros(total.shape, jnp.float32)

        @pl.loop(0, D // CHUNK)
        def _(chunk):
            dense = columns_out(where_ref, weights_ref, base, chunk * BLOCKS, BLOCKS)
            total[...] += dot(upstream_ref[:, columns(chunk)], dense, NT)

        pre = pre_ref[layer]
        sig = jax.nn.sigmoid(pre)
        dpre = (total[...] * sig * (1.0 + pre * (1.0 - sig))).astype(jnp.bfloat16)
        dpre_ref[...] = dpre
        mean = jnp.sum(dpre.astype(jnp.float32) * pre, axis=-1, keepdims=True) / D
        inner[...] = jnp.broadcast_to(mean, inner.shape)

    @pl.when(step == 1)
    def _():
        base = place * 2 * NBLK
        scale = scale_ref[layer][:, :1]
        mean = inner[:, :1]

        @pl.loop(0, D // CHUNK)
        def _(chunk):
            dense = rows_in(where_ref, weights_ref, base, chunk * BLOCKS, BLOCKS)
            dnorm = dot(dpre_ref[...], dense, NT)
            unit = hidden_ref[:, columns(chunk)].astype(jnp.float32) / scale
            earlier_ref[:, columns(chunk)] = (
                upstream_ref[:, columns(chunk)].astype(jnp.float32) + (dnorm - unit * mean) / scale
            ).astype(jnp.bfloat16)


def pick(places_ref, dense, out_ref, base):
    owners, slots = out_ref.shape[0], out_ref.shape[2]

    @pl.loop(0, owners)
    def _(owner):
        for slot in range(slots):
            out_ref[owner, 0, slot] = dense[places_ref[base + owner * slots + slot]]


def gradient_in_kernel(places_ref, own_ref, other_ref, dpre_own_ref, dpre_other_ref, out_ref, dense):
    step = pl.program_id(0)

    @pl.when(step == 0)
    def _():
        dense[NBLK] = jnp.zeros((BLOCK, BLOCK), jnp.bfloat16)

        @pl.loop(0, D // SPAN)
        def _(chunk):
            normed = jnp.concatenate([own_ref[:, columns(chunk, SPAN)], other_ref[:, columns(chunk, SPAN)]], axis=0)
            dpre = jnp.concatenate([dpre_own_ref[...], dpre_other_ref[...]], axis=0)
            part = dot(normed, dpre, TN).astype(jnp.bfloat16)
            for row in range(SPAN // BLOCK):
                for col in range(ROWS_K):
                    dense[(chunk * (SPAN // BLOCK) + row) * ROWS_K + col] = part[
                        row * BLOCK : (row + 1) * BLOCK, col * BLOCK : (col + 1) * BLOCK
                    ]

    pick(places_ref, dense, out_ref, step * out_ref.shape[0] * out_ref.shape[2])


def gradient_out_kernel(places_ref, _, act_own_ref, act_other_ref, own_ref, other_ref, out_ref, dense, turned):
    step = pl.program_id(0)

    @pl.when(step == 0)
    def _():
        dense[NBLK] = jnp.zeros((BLOCK, BLOCK), jnp.bfloat16)
        act = jnp.concatenate([act_own_ref[...], act_other_ref[...]], axis=0)
        turned[...] = act.astype(jnp.float32).T.astype(jnp.bfloat16)

        @pl.loop(0, D // SPAN)
        def _(chunk):
            upstream = jnp.concatenate([own_ref[:, columns(chunk, SPAN)], other_ref[:, columns(chunk, SPAN)]], axis=0)
            part = dot(turned[...], upstream, NN).astype(jnp.bfloat16)
            for row in range(ROWS_K):
                for col in range(SPAN // BLOCK):
                    dense[row * ROWS_D + chunk * (SPAN // BLOCK) + col] = part[
                        row * BLOCK : (row + 1) * BLOCK, col * BLOCK : (col + 1) * BLOCK
                    ]

    pick(places_ref, dense, out_ref, (places_ref.shape[0] // 2) + step * out_ref.shape[0] * out_ref.shape[2])


def whole(*shape):
    return pl.BlockSpec(shape, lambda step, *_: (0,) * len(shape))


def params(flops, moved):
    return dict(
        compiler_params=pltpu.CompilerParams(
            dimension_semantics=("arbitrary",), vmem_limit_bytes=56 * 1024 * 1024
        ),
        cost_estimate=pl.CostEstimate(flops=flops, bytes_accessed=moved, transcendentals=0),
    )


def swapped(array):
    return lax.ppermute(array, "section", PAIR)


def per_device(tokens, blocks_in, blocks_out, pos_in, pos_out, cotangent):
    here = lax.axis_index("section")
    owners = lax.axis_size("dp")
    slots = blocks_in.shape[1]
    rows = tokens.shape[0] // 2
    odd = here % 2
    swap = odd.astype(jnp.int32).reshape(1)
    upper = here >= 2
    half = jnp.where((here == 1) | (here == 2), rows, 0)

    own = jnp.stack([blocks_in[0], blocks_out[0]])
    weights = lax.all_gather(jnp.stack([own, swapped(own)]), "dp", axis=0)
    own_places = jnp.stack([pos_in[0], pos_out[0]])
    places = lax.all_gather(jnp.stack([own_places, swapped(own_places)]), "dp", axis=0).transpose(1, 2, 0, 3)
    codes = jnp.arange(owners, dtype=jnp.int32)[:, None] * 8 + jnp.arange(slots, dtype=jnp.int32)
    named = places[..., None] == jnp.arange(NBLK, dtype=jnp.int32)
    where = jnp.max(jnp.where(named, codes[..., None], -1), axis=(2, 3)).reshape(-1)
    places = places[0].reshape(-1)

    first_tokens = lax.dynamic_slice_in_dim(tokens, half, rows, 0)
    last_grads = lax.dynamic_slice_in_dim(cotangent, half, rows, 0)

    def shape(*dims, dtype=jnp.bfloat16):
        return jax.ShapeDtypeStruct(dims, dtype)

    piece = (owners, 1, 1, slots, BLOCK, BLOCK)
    moved = weights.size * 2
    work = 2 * rows * D * RANK

    forward = pl.pallas_call(
        forward_kernel,
        out_shape=(
            shape(rows, D),
            shape(rows, D),
            shape(2, rows, RANK, dtype=jnp.float32),
            shape(2, rows, BLOCK, dtype=jnp.float32),
            shape(2, rows, D),
            shape(2, rows, RANK),
        ),
        grid_spec=pltpu.PrefetchScalarGridSpec(
            num_scalar_prefetch=2,
            grid=(4,),
            in_specs=[
                whole(rows, D),
                pl.BlockSpec(piece, lambda step, swap, _: (0, (step // 2) ^ swap[0], step % 2, 0, 0, 0)),
            ],
            out_specs=[
                whole(rows, D),
                whole(rows, D),
                whole(2, rows, RANK),
                whole(2, rows, BLOCK),
                whole(2, rows, D),
                whole(2, rows, RANK),
            ],
        ),
        name="forward_layers",
        **params(4 * work, moved),
    )

    def backward(layer):
        return pl.pallas_call(
            functools.partial(backward_kernel, layer),
            out_shape=(shape(rows, D), shape(rows, RANK)),
            grid_spec=pltpu.PrefetchScalarGridSpec(
                num_scalar_prefetch=2,
                grid=(2,),
                in_specs=[
                    whole(rows, D),
                    whole(rows, D),
                    whole(2, rows, RANK),
                    whole(2, rows, BLOCK),
                    pl.BlockSpec(piece, lambda step, swap, _: (0, layer ^ swap[0], 1 - step, 0, 0, 0)),
                ],
                out_specs=[whole(rows, D), whole(rows, RANK)],
                scratch_shapes=[pltpu.VMEM((rows, RANK), jnp.float32), pltpu.VMEM((rows, BLOCK), jnp.float32)],
            ),
            name=f"backward_layer_{layer}",
            **params(2 * work, moved // 2),
        )

    steps = 4
    part = (owners // steps, 1, slots, BLOCK, BLOCK)
    partial_shape = shape(owners, 2, slots, BLOCK, BLOCK)
    dense = pltpu.VMEM((NBLK + 1, BLOCK, BLOCK), jnp.bfloat16)
    gradient_in = pl.pallas_call(
        gradient_in_kernel,
        out_shape=partial_shape,
        grid_spec=pltpu.PrefetchScalarGridSpec(
            num_scalar_prefetch=1,
            grid=(steps,),
            in_specs=[whole(rows, D), whole(rows, D), whole(rows, RANK), whole(rows, RANK)],
            out_specs=pl.BlockSpec(part, lambda step, _: (step, 0, 0, 0, 0)),
            scratch_shapes=[dense],
        ),
        name="gradient_in",
        **params(2 * work, moved // 4),
    )
    gradient_out = pl.pallas_call(
        gradient_out_kernel,
        out_shape=partial_shape,
        grid_spec=pltpu.PrefetchScalarGridSpec(
            num_scalar_prefetch=1,
            grid=(steps,),
            in_specs=[
                pl.BlockSpec(memory_space=pl.ANY),
                whole(rows, RANK),
                whole(rows, RANK),
                whole(rows, D),
                whole(rows, D),
            ],
            out_specs=pl.BlockSpec(part, lambda step, _: (step, 1, 0, 0, 0)),
            scratch_shapes=[dense, pltpu.VMEM((RANK, 2 * rows), jnp.bfloat16)],
        ),
        input_output_aliases={1: 0},
        name="gradient_out",
        **params(2 * work, moved // 4),
    )

    _, leaving, _, _, _, _ = forward(swap, where, first_tokens, weights)
    arrived = lax.ppermute(leaving, "section", UP)
    first = jnp.where(upper, arrived, first_tokens)
    second, _, pre, scale, normed, act = forward(swap, where, first, weights)
    normed_other = swapped(normed[1])
    act_other = swapped(act[1])

    middle, _ = backward(1)(swap, where, second, last_grads, pre, scale, weights)
    leaving, _ = backward(0)(swap, where, first, middle, pre, scale, weights)
    arrived = lax.ppermute(leaving, "section", DOWN)
    grads = jnp.where(upper, last_grads, arrived)
    middle, dpre_high = backward(1)(swap, where, second, grads, pre, scale, weights)
    grads_other = swapped(jnp.where(odd == 0, grads, middle))
    grads_own = jnp.where(odd == 0, middle, grads)
    _, dpre_low = backward(0)(swap, where, first, middle, pre, scale, weights)
    dpre_other = swapped(jnp.where(odd == 0, dpre_high, dpre_low))
    dpre_own = jnp.where(odd == 0, dpre_low, dpre_high)

    partial = gradient_in(places, normed[0], normed_other, dpre_own, dpre_other)
    partial = gradient_out(places, partial, act[0], act_other, grads_own, grads_other)
    summed = lax.psum_scatter(partial, "dp", scatter_dimension=0, tiled=False)
    return (summed[0][None], summed[1][None])


def solution(mesh):
    in_specs = (
        P("dp", None),
        P("section", "dp", None, None),
        P("section", "dp", None, None),
        P("section", "dp"),
        P("section", "dp"),
        P("dp", None),
    )
    out_specs = (P("section", "dp", None, None), P("section", "dp", None, None))
    return jax.shard_map(
        per_device, mesh=mesh, in_specs=in_specs, out_specs=out_specs, check_vma=False
    )
```

```python
import functools

import jax
import jax.numpy as jnp
from jax import lax
from jax.experimental import pallas as pl
from jax.experimental.pallas import tpu as pltpu
from jax.sharding import PartitionSpec as P

D = 8192
RANK = 512
BLOCK = 128
ROWS_D = D // BLOCK
ROWS_K = RANK // BLOCK
NBLK = ROWS_D * ROWS_K
EPS = 1e-05
CHUNK = 1024
BLOCKS = CHUNK // BLOCK
SPAN = 1024
NT = (((1,), (1,)), ((), ()))
NN = (((1,), (0,)), ((), ()))
TN = (((0,), (0,)), ((), ()))
PAIR = [(0, 1), (1, 0), (2, 3), (3, 2)]
UP = [(0, 3), (1, 2)]
DOWN = [(3, 0), (2, 1)]


def dot(left, right, dims):
    return lax.dot_general(left, right, dims, preferred_element_type=jnp.float32)


class Weights:
    def __init__(self, swap_ref, where_ref, source, held, sems, wanted):
        self.where_ref = where_ref
        self.swap = swap_ref[0]
        self.held = held
        self.order = wanted
        owners = source.shape[0]
        self.copies = {}
        for i, (layer, matrix) in enumerate(wanted):
            copy = pltpu.make_async_copy(source.at[:, layer ^ self.swap, matrix], held.at[i, pl.ds(0, owners)], sems.at[i])
            copy.start()
            self.copies[layer, matrix] = copy
        for i in range(len(wanted)):
            held[i, owners, 0] = jnp.zeros(held.shape[3:], held.dtype)

    def wait(self, layer, matrix):
        self.copies[layer, matrix].wait()

    def block(self, layer, matrix, number):
        code = self.where_ref[((layer ^ self.swap) * 2 + matrix) * NBLK + number]
        return self.held[self.order.index((layer, matrix)), code >> 3, code & 7]

    def rows_in(self, layer, chunk):
        rows = range(chunk * BLOCKS, (chunk + 1) * BLOCKS)
        return jnp.concatenate(
            [
                jnp.concatenate([self.block(layer, 0, row * ROWS_K + col) for col in range(ROWS_K)], axis=1)
                for row in rows
            ],
            axis=0,
        )

    def columns_out(self, layer, chunk):
        cols = range(chunk * BLOCKS, (chunk + 1) * BLOCKS)
        return jnp.concatenate(
            [
                jnp.concatenate([self.block(layer, 1, row * ROWS_D + col) for col in cols], axis=1)
                for row in range(ROWS_K)
            ],
            axis=0,
        )


def chunks():
    return [(chunk, slice(chunk * CHUNK, (chunk + 1) * CHUNK)) for chunk in range(D // CHUNK)]


def forward_down(weights, layer, hidden_ref, normed_ref):
    total = 0.0
    for _, cols in chunks():
        wide = hidden_ref[:, cols].astype(jnp.float32)
        total = total + jnp.sum(wide * wide, axis=-1, keepdims=True)
    inverse = 1.0 / jnp.sqrt(total / D + EPS)
    for _, cols in chunks():
        normed_ref[:, cols] = (hidden_ref[:, cols].astype(jnp.float32) * inverse).astype(jnp.bfloat16)
    weights.wait(layer, 0)
    pre = 0.0
    for chunk, cols in chunks():
        pre = pre + dot(normed_ref[:, cols], weights.rows_in(layer, chunk), NN)
    return pre, inverse


def forward_up(weights, layer, hidden_ref, act, next_ref):
    weights.wait(layer, 1)
    for chunk, cols in chunks():
        moved = dot(act, weights.columns_out(layer, chunk), NN)
        next_ref[:, cols] = (hidden_ref[:, cols].astype(jnp.float32) + moved).astype(jnp.bfloat16)


def backward(weights, layer, hidden_ref, upstream_ref, pre, inverse, earlier_ref):
    dact = 0.0
    for chunk, cols in chunks():
        dact = dact + dot(upstream_ref[:, cols], weights.columns_out(layer, chunk), NT)
    sig = jax.nn.sigmoid(pre)
    dpre = (dact * sig * (1.0 + pre * (1.0 - sig))).astype(jnp.bfloat16)
    if earlier_ref is not None:
        mean = jnp.sum(dpre.astype(jnp.float32) * pre, axis=-1, keepdims=True) / D
        pull = mean * inverse * inverse
        for chunk, cols in chunks():
            dnorm = dot(dpre, weights.rows_in(layer, chunk), NT)
            hidden = hidden_ref[:, cols].astype(jnp.float32)
            earlier_ref[:, cols] = (
                upstream_ref[:, cols].astype(jnp.float32) + dnorm * inverse - hidden * pull
            ).astype(jnp.bfloat16)
    return dpre


def silu(pre):
    return (pre * jax.nn.sigmoid(pre)).astype(jnp.bfloat16)


def forward_kernel(swap_ref, where_ref, first_ref, source, last_ref, second_ref, normed_ref, held, sems):
    weights = Weights(swap_ref, where_ref, source, held, sems, [(0, 0), (0, 1), (1, 0), (1, 1)])
    pre, _ = forward_down(weights, 0, first_ref, normed_ref)
    forward_up(weights, 0, first_ref, silu(pre), second_ref)
    pre, _ = forward_down(weights, 1, second_ref, normed_ref)
    forward_up(weights, 1, second_ref, silu(pre), last_ref)


def turn_kernel(
    swap_ref, where_ref, first_ref, grad_ref, source, second_ref, pre_ref, inverse_ref, normed_ref, act_ref, earlier_ref, middle_ref, held, sems
):
    weights = Weights(swap_ref, where_ref, source, held, sems, [(0, 0), (0, 1), (1, 0), (1, 1)])
    pres, inverses = [], []
    for layer, hidden_ref in enumerate((first_ref, second_ref)):
        place = layer ^ swap_ref[0]
        pre, inverse = forward_down(weights, layer, hidden_ref, normed_ref.at[place])
        act = silu(pre)
        pre_ref[layer] = pre
        inverse_ref[layer] = jnp.broadcast_to(inverse, inverse_ref.shape[1:])
        act_ref[place] = act
        if layer == 0:
            forward_up(weights, 0, first_ref, act, second_ref)
    weights.wait(1, 1)
    backward(weights, 1, second_ref, grad_ref, pre_ref[1], inverse_ref[1][:, :1], middle_ref)
    backward(weights, 0, first_ref, middle_ref, pre_ref[0], inverse_ref[0][:, :1], earlier_ref)


def backward_kernel(
    layer, last, swap_ref, where_ref, hidden_ref, upstream_ref, pre_ref, inverse_ref, source, *outs
):
    held, sems = outs[-2:]
    weights = Weights(swap_ref, where_ref, source, held, sems, [(layer, 1)] if last else [(layer, 1), (layer, 0)])
    for matrix in [1] if last else [1, 0]:
        weights.wait(layer, matrix)
    outs[0][...] = backward(
        weights, layer, hidden_ref, upstream_ref, pre_ref[layer], inverse_ref[layer][:, :1], None if last else outs[1]
    )


def pick(places_ref, dense, out_ref, base):
    owners, slots = out_ref.shape[0], out_ref.shape[2]

    for owner in range(owners):
        for slot in range(slots):
            out_ref[owner, 0, slot] = dense[places_ref[base + owner * slots + slot]]


def gradient_in_kernel(places_ref, own_ref, other_ref, dpre_own_ref, dpre_other_ref, out_ref, dense):
    step = pl.program_id(0)

    @pl.when(step == 0)
    def _():
        dense[NBLK] = jnp.zeros((BLOCK, BLOCK), jnp.bfloat16)

        dpre = jnp.concatenate([dpre_own_ref[...], dpre_other_ref[...]], axis=0)
        for chunk in range(D // SPAN):
            cols = slice(chunk * SPAN, (chunk + 1) * SPAN)
            normed = jnp.concatenate([own_ref[:, cols], other_ref[:, cols]], axis=0)
            part = dot(normed, dpre, TN).astype(jnp.bfloat16)
            for row in range(SPAN // BLOCK):
                for col in range(ROWS_K):
                    dense[(chunk * (SPAN // BLOCK) + row) * ROWS_K + col] = part[
                        row * BLOCK : (row + 1) * BLOCK, col * BLOCK : (col + 1) * BLOCK
                    ]

    pick(places_ref, dense, out_ref, step * out_ref.shape[0] * out_ref.shape[2])


def gradient_out_kernel(places_ref, _, act_own_ref, act_other_ref, own_ref, other_ref, out_ref, dense, turned):
    step = pl.program_id(0)

    @pl.when(step == 0)
    def _():
        dense[NBLK] = jnp.zeros((BLOCK, BLOCK), jnp.bfloat16)
        act = jnp.concatenate([act_own_ref[...], act_other_ref[...]], axis=0)
        turned[...] = act.astype(jnp.float32).T.astype(jnp.bfloat16)

        for chunk in range(D // SPAN):
            cols = slice(chunk * SPAN, (chunk + 1) * SPAN)
            upstream = jnp.concatenate([own_ref[:, cols], other_ref[:, cols]], axis=0)
            part = dot(turned[...], upstream, NN).astype(jnp.bfloat16)
            for row in range(ROWS_K):
                for col in range(SPAN // BLOCK):
                    dense[row * ROWS_D + chunk * (SPAN // BLOCK) + col] = part[
                        row * BLOCK : (row + 1) * BLOCK, col * BLOCK : (col + 1) * BLOCK
                    ]

    pick(places_ref, dense, out_ref, (places_ref.shape[0] // 2) + step * out_ref.shape[0] * out_ref.shape[2])


def whole(*shape):
    return pl.BlockSpec(shape, lambda step, *_: (0,) * len(shape))


def params(flops, moved):
    return dict(
        compiler_params=pltpu.CompilerParams(
            dimension_semantics=("arbitrary",), vmem_limit_bytes=56 * 1024 * 1024
        ),
        cost_estimate=pl.CostEstimate(flops=flops, bytes_accessed=moved, transcendentals=0),
    )


def swapped(array):
    return lax.ppermute(array, "section", PAIR)


def per_device(tokens, blocks_in, blocks_out, pos_in, pos_out, cotangent):
    here = lax.axis_index("section")
    owners = lax.axis_size("dp")
    slots = blocks_in.shape[1]
    rows = tokens.shape[0] // 2
    odd = here % 2
    swap = odd.astype(jnp.int32).reshape(1)
    upper = here >= 2
    half = jnp.where((here == 1) | (here == 2), rows, 0)

    own = jnp.stack([blocks_in[0], blocks_out[0]])
    weights = lax.all_gather(jnp.stack([own, swapped(own)]), "dp", axis=0)
    own_places = jnp.stack([pos_in[0], pos_out[0]])
    places = lax.all_gather(jnp.stack([own_places, swapped(own_places)]), "dp", axis=0).transpose(1, 2, 0, 3)
    codes = jnp.arange(owners, dtype=jnp.int32)[:, None] * 8 + jnp.arange(slots, dtype=jnp.int32)
    named = places[..., None] == jnp.arange(NBLK, dtype=jnp.int32)
    where = jnp.max(jnp.where(named, codes[..., None], -1), axis=(2, 3)).reshape(-1)
    where = jnp.where(where < 0, owners * 8, where)
    places = places[0].reshape(-1)

    first_tokens = lax.dynamic_slice_in_dim(tokens, half, rows, 0)
    last_grads = lax.dynamic_slice_in_dim(cotangent, half, rows, 0)

    def shape(*dims, dtype=jnp.bfloat16):
        return jax.ShapeDtypeStruct(dims, dtype)

    moved = weights.size * 2
    work = 2 * rows * D * RANK
    anywhere = pl.BlockSpec(memory_space=pl.ANY)

    def held(count):
        return [
            pltpu.VMEM((count, owners + 1, slots, BLOCK, BLOCK), jnp.bfloat16),
            pltpu.SemaphoreType.DMA((count,)),
        ]

    forward = pl.pallas_call(
        forward_kernel,
        out_shape=shape(rows, D),
        grid_spec=pltpu.PrefetchScalarGridSpec(
            num_scalar_prefetch=2,
            grid=(1,),
            in_specs=[whole(rows, D), anywhere],
            out_specs=whole(rows, D),
            scratch_shapes=[pltpu.VMEM((rows, D), jnp.bfloat16), pltpu.VMEM((rows, D), jnp.bfloat16)] + held(4),
        ),
        name="forward_layers",
        **params(4 * work, moved),
    )
    turn = pl.pallas_call(
        turn_kernel,
        out_shape=(
            shape(rows, D),
            shape(2, rows, RANK, dtype=jnp.float32),
            shape(2, rows, BLOCK, dtype=jnp.float32),
            shape(2, rows, D),
            shape(2, rows, RANK),
            shape(rows, D),
        ),
        grid_spec=pltpu.PrefetchScalarGridSpec(
            num_scalar_prefetch=2,
            grid=(1,),
            in_specs=[whole(rows, D), whole(rows, D), anywhere],
            out_specs=[
                whole(rows, D),
                whole(2, rows, RANK),
                whole(2, rows, BLOCK),
                whole(2, rows, D),
                whole(2, rows, RANK),
                whole(rows, D),
            ],
            scratch_shapes=[pltpu.VMEM((rows, D), jnp.bfloat16)] + held(4),
        ),
        name="turn_layers",
        **params(7 * work, moved),
    )

    def backward_layer(layer, last):
        return pl.pallas_call(
            functools.partial(backward_kernel, layer, last),
            out_shape=(shape(rows, RANK),) + (() if last else (shape(rows, D),)),
            grid_spec=pltpu.PrefetchScalarGridSpec(
                num_scalar_prefetch=2,
                grid=(1,),
                in_specs=[
                    whole(rows, D),
                    whole(rows, D),
                    whole(2, rows, RANK),
                    whole(2, rows, BLOCK),
                    anywhere,
                ],
                out_specs=[whole(rows, RANK)] + ([] if last else [whole(rows, D)]),
                scratch_shapes=held(1 if last else 2),
            ),
            name=f"backward_layer_{layer}",
            **params((1 if last else 2) * work, moved // 4 * (1 if last else 2)),
        )

    steps = 4
    part = (owners // steps, 1, slots, BLOCK, BLOCK)
    partial_shape = shape(owners, 2, slots, BLOCK, BLOCK)
    dense = pltpu.VMEM((NBLK + 1, BLOCK, BLOCK), jnp.bfloat16)
    gradient_in = pl.pallas_call(
        gradient_in_kernel,
        out_shape=partial_shape,
        grid_spec=pltpu.PrefetchScalarGridSpec(
            num_scalar_prefetch=1,
            grid=(steps,),
            in_specs=[whole(rows, D), whole(rows, D), whole(rows, RANK), whole(rows, RANK)],
            out_specs=pl.BlockSpec(part, lambda step, _: (step, 0, 0, 0, 0)),
            scratch_shapes=[dense],
        ),
        name="gradient_in",
        **params(2 * work, moved // 4),
    )
    gradient_out = pl.pallas_call(
        gradient_out_kernel,
        out_shape=partial_shape,
        grid_spec=pltpu.PrefetchScalarGridSpec(
            num_scalar_prefetch=1,
            grid=(steps,),
            in_specs=[
                pl.BlockSpec(memory_space=pl.ANY),
                whole(rows, RANK),
                whole(rows, RANK),
                whole(rows, D),
                whole(rows, D),
            ],
            out_specs=pl.BlockSpec(part, lambda step, _: (step, 1, 0, 0, 0)),
            scratch_shapes=[dense, pltpu.VMEM((RANK, 2 * rows), jnp.bfloat16)],
        ),
        input_output_aliases={1: 0},
        name="gradient_out",
        **params(2 * work, moved // 4),
    )

    arrived = lax.ppermute(forward(swap, where, first_tokens, weights), "section", UP)
    first = jnp.where(upper, arrived, first_tokens)
    second, pre, inverse, normed, act, leaving = turn(swap, where, first, last_grads, weights)
    arrived = lax.ppermute(leaving, "section", DOWN)
    normed_other = swapped(normed[1])
    act_other = swapped(act[1])

    grads = jnp.where(upper, last_grads, arrived)
    dpre_high, middle = backward_layer(1, False)(swap, where, second, grads, pre, inverse, weights)
    grads_other = swapped(jnp.where(odd == 0, grads, middle))
    grads_own = jnp.where(odd == 0, middle, grads)
    (dpre_low,) = backward_layer(0, True)(swap, where, first, middle, pre, inverse, weights)
    dpre_other = swapped(jnp.where(odd == 0, dpre_high, dpre_low))
    dpre_own = jnp.where(odd == 0, dpre_low, dpre_high)

    partial = gradient_in(places, normed[0], normed_other, dpre_own, dpre_other)
    partial = gradient_out(places, partial, act[0], act_other, grads_own, grads_other)
    summed = lax.psum_scatter(partial, "dp", scatter_dimension=0, tiled=False)
    return (summed[0][None], summed[1][None])


def solution(mesh):
    in_specs = (
        P("dp", None),
        P("section", "dp", None, None),
        P("section", "dp", None, None),
        P("section", "dp"),
        P("section", "dp"),
        P("dp", None),
    )
    out_specs = (P("section", "dp", None, None), P("section", "dp", None, None))
    return jax.shard_map(
        per_device, mesh=mesh, in_specs=in_specs, out_specs=out_specs, check_vma=False
    )
```

```python
import functools

import jax
import jax.numpy as jnp
from jax import lax
from jax.experimental import pallas as pl
from jax.experimental.pallas import tpu as pltpu
from jax.sharding import PartitionSpec as P

D = 8192
RANK = 512
BLOCK = 128
ROWS_D = D // BLOCK
ROWS_K = RANK // BLOCK
NBLK = ROWS_D * ROWS_K
EPS = 1e-05
CHUNK = 1024
BLOCKS = CHUNK // BLOCK
NT = (((1,), (1,)), ((), ()))
NN = (((1,), (0,)), ((), ()))
TN = (((0,), (0,)), ((), ()))
PAIR = [(0, 1), (1, 0), (2, 3), (3, 2)]
UP = [(0, 3), (1, 2)]
DOWN = [(3, 0), (2, 1)]
RING = 4
Y = 2
Z = 8
CORES = [(i, i ^ 1) for i in range(Z * RING)]


def dot(left, right, dims):
    return lax.dot_general(left, right, dims, preferred_element_type=jnp.float32)


class Weights:
    def __init__(self, swap_ref, where_ref, source, held, sems, wanted):
        self.where_ref = where_ref
        self.swap = swap_ref[0]
        self.held = held
        self.order = wanted
        owners = source.shape[0]
        self.copies = {}
        for i, (layer, matrix) in enumerate(wanted):
            copy = pltpu.make_async_copy(source.at[:, layer ^ self.swap, matrix], held.at[i, pl.ds(0, owners)], sems.at[i])
            copy.start()
            self.copies[layer, matrix] = copy
        for i in range(len(wanted)):
            held[i, owners, 0] = jnp.zeros(held.shape[3:], held.dtype)

    def wait(self, layer, matrix):
        self.copies[layer, matrix].wait()

    def block(self, layer, matrix, number):
        code = self.where_ref[((layer ^ self.swap) * 2 + matrix) * NBLK + number]
        return self.held[self.order.index((layer, matrix)), code >> 3, code & 7]

    def rows_in(self, layer, chunk):
        rows = range(chunk * BLOCKS, (chunk + 1) * BLOCKS)
        return jnp.concatenate(
            [
                jnp.concatenate([self.block(layer, 0, row * ROWS_K + col) for col in range(ROWS_K)], axis=1)
                for row in rows
            ],
            axis=0,
        )

    def columns_out(self, layer, chunk):
        cols = range(chunk * BLOCKS, (chunk + 1) * BLOCKS)
        return jnp.concatenate(
            [
                jnp.concatenate([self.block(layer, 1, row * ROWS_D + col) for col in cols], axis=1)
                for row in range(ROWS_K)
            ],
            axis=0,
        )


def chunks():
    return [(chunk, slice(chunk * CHUNK, (chunk + 1) * CHUNK)) for chunk in range(D // CHUNK)]


def forward_down(weights, layer, hidden_ref, normed_ref):
    total = 0.0
    for _, cols in chunks():
        wide = hidden_ref[:, cols].astype(jnp.float32)
        total = total + jnp.sum(wide * wide, axis=-1, keepdims=True)
    inverse = 1.0 / jnp.sqrt(total / D + EPS)
    for _, cols in chunks():
        normed_ref[:, cols] = (hidden_ref[:, cols].astype(jnp.float32) * inverse).astype(jnp.bfloat16)
    weights.wait(layer, 0)
    pre = 0.0
    for chunk, cols in chunks():
        pre = pre + dot(normed_ref[:, cols], weights.rows_in(layer, chunk), NN)
    return pre, inverse


def forward_up(weights, layer, hidden_ref, act, next_ref):
    weights.wait(layer, 1)
    for chunk, cols in chunks():
        moved = dot(act, weights.columns_out(layer, chunk), NN)
        next_ref[:, cols] = (hidden_ref[:, cols].astype(jnp.float32) + moved).astype(jnp.bfloat16)


def backward(weights, layer, hidden_ref, upstream_ref, pre, inverse, earlier_ref):
    dact = 0.0
    for chunk, cols in chunks():
        dact = dact + dot(upstream_ref[:, cols], weights.columns_out(layer, chunk), NT)
    sig = jax.nn.sigmoid(pre)
    dpre = (dact * sig * (1.0 + pre * (1.0 - sig))).astype(jnp.bfloat16)
    if earlier_ref is not None:
        mean = jnp.sum(dpre.astype(jnp.float32) * pre, axis=-1, keepdims=True) / D
        pull = mean * inverse * inverse
        for chunk, cols in chunks():
            dnorm = dot(dpre, weights.rows_in(layer, chunk), NT)
            hidden = hidden_ref[:, cols].astype(jnp.float32)
            earlier_ref[:, cols] = (
                upstream_ref[:, cols].astype(jnp.float32) + dnorm * inverse - hidden * pull
            ).astype(jnp.bfloat16)
    return dpre


def silu(pre):
    return (pre * jax.nn.sigmoid(pre)).astype(jnp.bfloat16)


def forward_kernel(swap_ref, where_ref, first_ref, source, last_ref, second_ref, normed_ref, held, sems):
    weights = Weights(swap_ref, where_ref, source, held, sems, [(0, 0), (0, 1), (1, 0), (1, 1)])
    pre, _ = forward_down(weights, 0, first_ref, normed_ref)
    forward_up(weights, 0, first_ref, silu(pre), second_ref)
    pre, _ = forward_down(weights, 1, second_ref, normed_ref)
    forward_up(weights, 1, second_ref, silu(pre), last_ref)


def turn_kernel(
    swap_ref, where_ref, first_ref, grad_ref, source, second_ref, pre_ref, inverse_ref, normed_ref, act_ref, earlier_ref, middle_ref, held, sems
):
    weights = Weights(swap_ref, where_ref, source, held, sems, [(0, 0), (0, 1), (1, 0), (1, 1)])
    pres, inverses = [], []
    for layer, hidden_ref in enumerate((first_ref, second_ref)):
        place = layer ^ swap_ref[0]
        pre, inverse = forward_down(weights, layer, hidden_ref, normed_ref.at[place])
        act = silu(pre)
        pre_ref[layer] = pre
        inverse_ref[layer] = jnp.broadcast_to(inverse, inverse_ref.shape[1:])
        act_ref[place] = act
        if layer == 0:
            forward_up(weights, 0, first_ref, act, second_ref)
    weights.wait(1, 1)
    backward(weights, 1, second_ref, grad_ref, pre_ref[1], inverse_ref[1][:, :1], middle_ref)
    backward(weights, 0, first_ref, middle_ref, pre_ref[0], inverse_ref[0][:, :1], earlier_ref)


def backward_kernel(
    layer, last, swap_ref, where_ref, hidden_ref, upstream_ref, pre_ref, inverse_ref, source, *outs
):
    held, sems = outs[-2:]
    weights = Weights(swap_ref, where_ref, source, held, sems, [(layer, 1)] if last else [(layer, 1), (layer, 0)])
    for matrix in [1] if last else [1, 0]:
        weights.wait(layer, matrix)
    outs[0][...] = backward(
        weights, layer, hidden_ref, upstream_ref, pre_ref[layer], inverse_ref[layer][:, :1], None if last else outs[1]
    )


def pick(places_ref, dense, keep_ref, send_ref):
    step = pl.program_id(0)
    pieces, slots = keep_ref.shape[1], keep_ref.shape[2]
    count = places_ref.shape[0] // 2
    for half, out_ref in enumerate((keep_ref, send_ref)):
        for piece in range(pieces):
            for slot in range(slots):
                index = half * count + step * pieces * slots + piece * slots + slot
                out_ref[0, piece, slot] = dense[places_ref[index]]


def gradient_in_kernel(places_ref, own_ref, other_ref, dpre_own_ref, dpre_other_ref, keep_ref, send_ref, dense):
    @pl.when(pl.program_id(0) == 0)
    def _():
        dense[NBLK] = jnp.zeros((BLOCK, BLOCK), jnp.bfloat16)
        dpre = jnp.concatenate([dpre_own_ref[...], dpre_other_ref[...]], axis=0)
        for chunk, cols in chunks():
            normed = jnp.concatenate([own_ref[:, cols], other_ref[:, cols]], axis=0)
            part = dot(normed, dpre, TN).astype(jnp.bfloat16)
            for row in range(BLOCKS):
                for col in range(ROWS_K):
                    dense[(chunk * BLOCKS + row) * ROWS_K + col] = part[
                        row * BLOCK : (row + 1) * BLOCK, col * BLOCK : (col + 1) * BLOCK
                    ]

    pick(places_ref, dense, keep_ref, send_ref)


def gradient_out_kernel(places_ref, act_own_ref, act_other_ref, own_ref, other_ref, keep_ref, send_ref, dense, turned):
    @pl.when(pl.program_id(0) == 0)
    def _():
        dense[NBLK] = jnp.zeros((BLOCK, BLOCK), jnp.bfloat16)
        act = jnp.concatenate([act_own_ref[...], act_other_ref[...]], axis=0)
        turned[...] = act.astype(jnp.float32).T.astype(jnp.bfloat16)
        for chunk, cols in chunks():
            upstream = jnp.concatenate([own_ref[:, cols], other_ref[:, cols]], axis=0)
            part = dot(turned[...], upstream, NN).astype(jnp.bfloat16)
            for row in range(ROWS_K):
                for col in range(BLOCKS):
                    dense[row * ROWS_D + chunk * BLOCKS + col] = part[
                        row * BLOCK : (row + 1) * BLOCK, col * BLOCK : (col + 1) * BLOCK
                    ]

    pick(places_ref, dense, keep_ref, send_ref)


def pair_sum_kernel(keep_ref, arrived_ref, *outs):
    for piece, out_ref in enumerate(outs):
        total = keep_ref[piece, 0].astype(jnp.float32) + arrived_ref[piece, 0].astype(jnp.float32)
        out_ref[0] = total.astype(jnp.bfloat16)


def ring_sum_kernel(*refs):
    terms, outs = refs[:RING], refs[RING:]
    for piece, out_ref in enumerate(outs):
        total = terms[0][piece].astype(jnp.float32)
        for term in terms[1:]:
            total = total + term[piece].astype(jnp.float32)
        out_ref[...] = total.astype(jnp.bfloat16)


def whole(*shape):
    return pl.BlockSpec(shape, lambda step, *_: (0,) * len(shape))


def params(flops, moved):
    return dict(
        compiler_params=pltpu.CompilerParams(
            dimension_semantics=("arbitrary",), vmem_limit_bytes=56 * 1024 * 1024
        ),
        cost_estimate=pl.CostEstimate(flops=flops, bytes_accessed=moved, transcendentals=0),
    )


def turn_axis(array, axis, start):
    size = array.shape[axis]
    return lax.dynamic_slice_in_dim(jnp.concatenate([array, array], axis), start, size, axis)


def around(array, stride, distance):
    if distance == 0:
        return array
    route = []
    for i in range(lax.axis_size("dp")):
        place = i // stride % RING
        route.append((i, i + ((place + distance) % RING - place) * stride))
    return lax.ppermute(array, "dp", route)


def swapped(array):
    return lax.ppermute(array, "section", PAIR)


def per_device(tokens, blocks_in, blocks_out, pos_in, pos_out, cotangent):
    here = lax.axis_index("section")
    owners = lax.axis_size("dp")
    slots = blocks_in.shape[1]
    rows = tokens.shape[0] // 2
    odd = here % 2
    swap = odd.astype(jnp.int32).reshape(1)
    upper = here >= 2
    half = jnp.where((here == 1) | (here == 2), rows, 0)

    own = jnp.stack([blocks_in[0], blocks_out[0]])
    weights = lax.all_gather(jnp.stack([own, swapped(own)]), "dp", axis=0)
    own_places = jnp.stack([pos_in[0], pos_out[0]])
    places = lax.all_gather(jnp.stack([own_places, swapped(own_places)]), "dp", axis=0).transpose(1, 2, 0, 3)
    codes = jnp.arange(owners, dtype=jnp.int32)[:, None] * 8 + jnp.arange(slots, dtype=jnp.int32)
    named = places[..., None] == jnp.arange(NBLK, dtype=jnp.int32)
    where = jnp.max(jnp.where(named, codes[..., None], -1), axis=(2, 3)).reshape(-1)
    where = jnp.where(where < 0, owners * 8, where)
    me = lax.axis_index("dp")
    mine = places[0].reshape(2, RING, RING, 2, slots)
    mine = turn_axis(mine, 1, me // Z)
    mine = turn_axis(mine, 2, (me // Y) % RING)
    mine = turn_axis(mine, 3, me % Y)
    places_in = mine[0].transpose(2, 1, 0, 3).reshape(-1)
    places_out = mine[1].transpose(2, 0, 1, 3).reshape(-1)

    first_tokens = lax.dynamic_slice_in_dim(tokens, half, rows, 0)
    last_grads = lax.dynamic_slice_in_dim(cotangent, half, rows, 0)

    def shape(*dims, dtype=jnp.bfloat16):
        return jax.ShapeDtypeStruct(dims, dtype)

    moved = weights.size * 2
    work = 2 * rows * D * RANK
    anywhere = pl.BlockSpec(memory_space=pl.ANY)

    def held(count):
        return [
            pltpu.VMEM((count, owners + 1, slots, BLOCK, BLOCK), jnp.bfloat16),
            pltpu.SemaphoreType.DMA((count,)),
        ]

    forward = pl.pallas_call(
        forward_kernel,
        out_shape=shape(rows, D),
        grid_spec=pltpu.PrefetchScalarGridSpec(
            num_scalar_prefetch=2,
            grid=(1,),
            in_specs=[whole(rows, D), anywhere],
            out_specs=whole(rows, D),
            scratch_shapes=[pltpu.VMEM((rows, D), jnp.bfloat16), pltpu.VMEM((rows, D), jnp.bfloat16)] + held(4),
        ),
        name="forward_layers",
        **params(4 * work, moved),
    )
    turn = pl.pallas_call(
        turn_kernel,
        out_shape=(
            shape(rows, D),
            shape(2, rows, RANK, dtype=jnp.float32),
            shape(2, rows, BLOCK, dtype=jnp.float32),
            shape(2, rows, D),
            shape(2, rows, RANK),
            shape(rows, D),
        ),
        grid_spec=pltpu.PrefetchScalarGridSpec(
            num_scalar_prefetch=2,
            grid=(1,),
            in_specs=[whole(rows, D), whole(rows, D), anywhere],
            out_specs=[
                whole(rows, D),
                whole(2, rows, RANK),
                whole(2, rows, BLOCK),
                whole(2, rows, D),
                whole(2, rows, RANK),
                whole(rows, D),
            ],
            scratch_shapes=[pltpu.VMEM((rows, D), jnp.bfloat16)] + held(4),
        ),
        name="turn_layers",
        **params(7 * work, moved),
    )

    def backward_layer(layer, last):
        return pl.pallas_call(
            functools.partial(backward_kernel, layer, last),
            out_shape=(shape(rows, RANK),) + (() if last else (shape(rows, D),)),
            grid_spec=pltpu.PrefetchScalarGridSpec(
                num_scalar_prefetch=2,
                grid=(1,),
                in_specs=[
                    whole(rows, D),
                    whole(rows, D),
                    whole(2, rows, RANK),
                    whole(2, rows, BLOCK),
                    anywhere,
                ],
                out_specs=[whole(rows, RANK)] + ([] if last else [whole(rows, D)]),
                scratch_shapes=held(1 if last else 2),
            ),
            name=f"backward_layer_{layer}",
            **params((1 if last else 2) * work, moved // 4 * (1 if last else 2)),
        )

    halves = shape(RING, RING, slots, BLOCK, BLOCK)
    half_spec = pl.BlockSpec((1, RING, slots, BLOCK, BLOCK), lambda step, _: (step, 0, 0, 0, 0))
    dense = pltpu.VMEM((NBLK + 1, BLOCK, BLOCK), jnp.bfloat16)

    def gradient(kernel, name, in_specs, scratch):
        return pl.pallas_call(
            kernel,
            out_shape=(halves, halves),
            grid_spec=pltpu.PrefetchScalarGridSpec(
                num_scalar_prefetch=1,
                grid=(RING,),
                in_specs=in_specs,
                out_specs=(half_spec, half_spec),
                scratch_shapes=[dense] + scratch,
            ),
            name=name,
            **params(2 * work, moved // 4),
        )

    gradient_in = gradient(
        gradient_in_kernel, "gradient_in", [whole(rows, D)] * 2 + [whole(rows, RANK)] * 2, []
    )
    gradient_out = gradient(
        gradient_out_kernel,
        "gradient_out",
        [whole(rows, RANK)] * 2 + [whole(rows, D)] * 2,
        [pltpu.VMEM((RANK, 2 * rows), jnp.bfloat16)],
    )
    column_spec = pl.BlockSpec((RING, 1, slots, BLOCK, BLOCK), lambda step: (0, step, 0, 0, 0))
    pair_sum = pl.pallas_call(
        pair_sum_kernel,
        out_shape=(shape(RING, slots, BLOCK, BLOCK),) * RING,
        grid=(RING,),
        in_specs=[column_spec] * 2,
        out_specs=(pl.BlockSpec((1, slots, BLOCK, BLOCK), lambda step: (step, 0, 0, 0)),) * RING,
        name="pair_sum",
        **params(0, moved // 5),
    )
    ring_sum = pl.pallas_call(
        ring_sum_kernel,
        out_shape=(shape(slots, BLOCK, BLOCK),) * RING,
        grid=(1,),
        in_specs=[whole(RING, slots, BLOCK, BLOCK)] * RING,
        out_specs=(whole(slots, BLOCK, BLOCK),) * RING,
        name="ring_sum",
        **params(0, moved // 8),
    )

    def scattered(gradient_halves, near, far):
        keep, send = gradient_halves
        pieces = pair_sum(keep, lax.ppermute(send, "dp", CORES))
        pieces = ring_sum(*[around(piece, near, distance) for distance, piece in enumerate(pieces)])
        terms = [around(piece, far, distance).astype(jnp.float32) for distance, piece in enumerate(pieces)]
        return sum(terms).astype(jnp.bfloat16)[None]

    arrived = lax.ppermute(forward(swap, where, first_tokens, weights), "section", UP)
    first = jnp.where(upper, arrived, first_tokens)
    second, pre, inverse, normed, act, leaving = turn(swap, where, first, last_grads, weights)
    arrived = lax.ppermute(leaving, "section", DOWN)
    normed_other = swapped(normed[1])
    act_other = swapped(act[1])

    grads = jnp.where(upper, last_grads, arrived)
    dpre_high, middle = backward_layer(1, False)(swap, where, second, grads, pre, inverse, weights)
    grads_other = swapped(jnp.where(odd == 0, grads, middle))
    grads_own = jnp.where(odd == 0, middle, grads)
    (dpre_low,) = backward_layer(0, True)(swap, where, first, middle, pre, inverse, weights)
    dpre_other = swapped(jnp.where(odd == 0, dpre_high, dpre_low))
    dpre_own = jnp.where(odd == 0, dpre_low, dpre_high)

    sums_in = scattered(gradient_in(places_in, normed[0], normed_other, dpre_own, dpre_other), Y, Z)
    sums_out = scattered(gradient_out(places_out, act[0], act_other, grads_own, grads_other), Z, Y)
    return (sums_in, sums_out)


def solution(mesh):
    in_specs = (
        P("dp", None),
        P("section", "dp", None, None),
        P("section", "dp", None, None),
        P("section", "dp"),
        P("section", "dp"),
        P("dp", None),
    )
    out_specs = (P("section", "dp", None, None), P("section", "dp", None, None))
    return jax.shard_map(
        per_device, mesh=mesh, in_specs=in_specs, out_specs=out_specs, check_vma=False
    )
```

```python
import functools

import jax
import jax.numpy as jnp
from jax import lax
from jax.experimental import pallas as pl
from jax.experimental.pallas import tpu as pltpu
from jax.sharding import PartitionSpec as P

D = 8192
RANK = 512
BLOCK = 128
ROWS_D = D // BLOCK
ROWS_K = RANK // BLOCK
NBLK = ROWS_D * ROWS_K
EPS = 1e-05
CHUNK = 1024
BLOCKS = CHUNK // BLOCK
NT = (((1,), (1,)), ((), ()))
NN = (((1,), (0,)), ((), ()))
TN = (((0,), (0,)), ((), ()))
PAIR = [(0, 1), (1, 0), (2, 3), (3, 2)]
UP = [(0, 3), (1, 2)]
DOWN = [(3, 0), (2, 1)]
RING = 4
Y = 2
Z = 8
CORES = [(i, i ^ 1) for i in range(Z * RING)]


def dot(left, right, dims):
    return lax.dot_general(left, right, dims, preferred_element_type=jnp.float32)


class Weights:
    def __init__(self, swap_ref, where_ref, source, held, sems, wanted):
        self.where_ref = where_ref
        self.swap = swap_ref[0]
        self.held = held
        self.order = wanted
        owners = source.shape[0]
        self.copies = {}
        for i, (layer, matrix) in enumerate(wanted):
            copy = pltpu.make_async_copy(source.at[:, layer ^ self.swap, matrix], held.at[i, pl.ds(0, owners)], sems.at[i])
            copy.start()
            self.copies[layer, matrix] = copy
        for i in range(len(wanted)):
            held[i, owners, 0] = jnp.zeros(held.shape[3:], held.dtype)

    def wait(self, layer, matrix):
        self.copies[layer, matrix].wait()

    def block(self, layer, matrix, number):
        code = self.where_ref[((layer ^ self.swap) * 2 + matrix) * NBLK + number]
        return self.held[self.order.index((layer, matrix)), code >> 3, code & 7]

    def rows_in(self, layer, chunk):
        rows = range(chunk * BLOCKS, (chunk + 1) * BLOCKS)
        return jnp.concatenate(
            [
                jnp.concatenate([self.block(layer, 0, row * ROWS_K + col) for col in range(ROWS_K)], axis=1)
                for row in rows
            ],
            axis=0,
        )

    def columns_out(self, layer, chunk):
        cols = range(chunk * BLOCKS, (chunk + 1) * BLOCKS)
        return jnp.concatenate(
            [
                jnp.concatenate([self.block(layer, 1, row * ROWS_D + col) for col in cols], axis=1)
                for row in range(ROWS_K)
            ],
            axis=0,
        )


def chunks():
    return [(chunk, slice(chunk * CHUNK, (chunk + 1) * CHUNK)) for chunk in range(D // CHUNK)]


def forward_down(weights, layer, hidden_ref, normed_ref):
    total = 0.0
    for _, cols in chunks():
        wide = hidden_ref[:, cols].astype(jnp.float32)
        total = total + jnp.sum(wide * wide, axis=-1, keepdims=True)
    inverse = 1.0 / jnp.sqrt(total / D + EPS)
    for _, cols in chunks():
        normed_ref[:, cols] = (hidden_ref[:, cols].astype(jnp.float32) * inverse).astype(jnp.bfloat16)
    weights.wait(layer, 0)
    pre = 0.0
    for chunk, cols in chunks():
        pre = pre + dot(normed_ref[:, cols], weights.rows_in(layer, chunk), NN)
    return pre, inverse


def forward_up(weights, layer, hidden_ref, act, next_ref):
    weights.wait(layer, 1)
    for chunk, cols in chunks():
        moved = dot(act, weights.columns_out(layer, chunk), NN)
        next_ref[:, cols] = (hidden_ref[:, cols].astype(jnp.float32) + moved).astype(jnp.bfloat16)


def backward(weights, layer, hidden_ref, upstream_ref, pre, inverse, earlier_ref):
    dact = 0.0
    for chunk, cols in chunks():
        dact = dact + dot(upstream_ref[:, cols], weights.columns_out(layer, chunk), NT)
    sig = jax.nn.sigmoid(pre)
    dpre = (dact * sig * (1.0 + pre * (1.0 - sig))).astype(jnp.bfloat16)
    if earlier_ref is not None:
        mean = jnp.sum(dpre.astype(jnp.float32) * pre, axis=-1, keepdims=True) / D
        pull = mean * inverse * inverse
        for chunk, cols in chunks():
            dnorm = dot(dpre, weights.rows_in(layer, chunk), NT)
            hidden = hidden_ref[:, cols].astype(jnp.float32)
            earlier_ref[:, cols] = (
                upstream_ref[:, cols].astype(jnp.float32) + dnorm * inverse - hidden * pull
            ).astype(jnp.bfloat16)
    return dpre


def silu(pre):
    return (pre * jax.nn.sigmoid(pre)).astype(jnp.bfloat16)


def forward_kernel(swap_ref, where_ref, first_ref, source, last_ref, second_ref, normed_ref, held, sems):
    weights = Weights(swap_ref, where_ref, source, held, sems, [(0, 0), (0, 1), (1, 0), (1, 1)])
    pre, _ = forward_down(weights, 0, first_ref, normed_ref)
    forward_up(weights, 0, first_ref, silu(pre), second_ref)
    pre, _ = forward_down(weights, 1, second_ref, normed_ref)
    forward_up(weights, 1, second_ref, silu(pre), last_ref)


def turn_kernel(
    swap_ref, where_ref, tokens_ref, arrived_ref, grad_ref, source, second_ref, pre_ref, inverse_ref, normed_ref, act_ref, earlier_ref, first_ref, middle_ref, held, sems
):
    weights = Weights(swap_ref, where_ref, source, held, sems, [(0, 0), (0, 1), (1, 0), (1, 1)])
    for _, cols in chunks():
        first_ref[:, cols] = lax.select(swap_ref[1] > 0, arrived_ref[:, cols], tokens_ref[:, cols])
    for layer, hidden_ref in enumerate((first_ref, second_ref)):
        place = layer ^ swap_ref[0]
        pre, inverse = forward_down(weights, layer, hidden_ref, normed_ref.at[place])
        act = silu(pre)
        pre_ref[layer] = pre
        inverse_ref[layer] = jnp.broadcast_to(inverse, inverse_ref.shape[1:])
        act_ref[place] = act
        if layer == 0:
            forward_up(weights, 0, first_ref, act, second_ref)
    weights.wait(1, 1)
    backward(weights, 1, second_ref, grad_ref, pre_ref[1], inverse_ref[1][:, :1], middle_ref)
    backward(weights, 0, first_ref, middle_ref, pre_ref[0], inverse_ref[0][:, :1], earlier_ref)


def high_kernel(
    swap_ref, where_ref, hidden_ref, grad_ref, arrived_ref, pre_ref, inverse_ref, source, dpre_ref, middle_ref, own_ref, early_ref, late_ref, upstream_ref, held, sems
):
    weights = Weights(swap_ref, where_ref, source, held, sems, [(1, 1), (1, 0)])
    rows = early_ref.shape[0]
    even = swap_ref[0] == 0
    for _, cols in chunks():
        upstream_ref[:, cols] = lax.select(swap_ref[1] > 0, grad_ref[:, cols], arrived_ref[:, cols])
    weights.wait(1, 1)
    weights.wait(1, 0)
    dpre_ref[...] = backward(weights, 1, hidden_ref, upstream_ref, pre_ref[1], inverse_ref[1][:, :1], middle_ref)
    for _, cols in chunks():
        upper, lower = upstream_ref[:, cols], middle_ref[:, cols]
        own_ref[:, cols] = lax.select(even, lower, upper)
        sent = lax.select(even, upper, lower)
        early_ref[:, cols] = sent[:rows]
        late_ref[:, cols] = sent[rows:]


def low_kernel(swap_ref, where_ref, middle_ref, high_ref, pre_ref, source, own_ref, sent_ref, held, sems):
    weights = Weights(swap_ref, where_ref, source, held, sems, [(0, 1)])
    even = swap_ref[0] == 0
    weights.wait(0, 1)
    low = backward(weights, 0, None, middle_ref, pre_ref[0], None, None)
    high = high_ref[...]
    own_ref[...] = lax.select(even, low, high)
    sent_ref[...] = lax.select(even, high, low)


def pick(places_ref, dense, keep_ref, send_ref):
    step = pl.program_id(0)
    pieces, slots = keep_ref.shape[1], keep_ref.shape[2]
    count = places_ref.shape[0] // 2
    for half, out_ref in enumerate((keep_ref, send_ref)):
        for piece in range(pieces):
            for slot in range(slots):
                index = half * count + step * pieces * slots + piece * slots + slot
                out_ref[0, piece, slot] = dense[places_ref[index]]


def gradient_in_kernel(places_ref, own_ref, other_ref, dpre_own_ref, dpre_other_ref, keep_ref, send_ref, dense):
    @pl.when(pl.program_id(0) == 0)
    def _():
        dense[NBLK] = jnp.zeros((BLOCK, BLOCK), jnp.bfloat16)
        dpre = jnp.concatenate([dpre_own_ref[...], dpre_other_ref[...]], axis=0)
        for chunk, cols in chunks():
            normed = jnp.concatenate([own_ref[:, cols], other_ref[:, cols]], axis=0)
            part = dot(normed, dpre, TN).astype(jnp.bfloat16)
            for row in range(BLOCKS):
                for col in range(ROWS_K):
                    dense[(chunk * BLOCKS + row) * ROWS_K + col] = part[
                        row * BLOCK : (row + 1) * BLOCK, col * BLOCK : (col + 1) * BLOCK
                    ]

    pick(places_ref, dense, keep_ref, send_ref)


def gradient_out_kernel(
    places_ref, act_own_ref, act_other_ref, own_ref, early_ref, late_ref, keep_ref, send_ref, dense, turned
):
    @pl.when(pl.program_id(0) == 0)
    def _():
        dense[NBLK] = jnp.zeros((BLOCK, BLOCK), jnp.bfloat16)
        act = jnp.concatenate([act_own_ref[...], act_other_ref[...]], axis=0)
        turned[...] = act.astype(jnp.float32).T.astype(jnp.bfloat16)
        for chunk, cols in chunks():
            upstream = jnp.concatenate([own_ref[:, cols], early_ref[:, cols], late_ref[:, cols]], axis=0)
            part = dot(turned[...], upstream, NN).astype(jnp.bfloat16)
            for row in range(ROWS_K):
                for col in range(BLOCKS):
                    dense[row * ROWS_D + chunk * BLOCKS + col] = part[
                        row * BLOCK : (row + 1) * BLOCK, col * BLOCK : (col + 1) * BLOCK
                    ]

    pick(places_ref, dense, keep_ref, send_ref)


def whole(*shape):
    return pl.BlockSpec(shape, lambda step, *_: (0,) * len(shape))


def params(flops, moved):
    return dict(
        compiler_params=pltpu.CompilerParams(
            dimension_semantics=("arbitrary",), vmem_limit_bytes=56 * 1024 * 1024
        ),
        cost_estimate=pl.CostEstimate(flops=flops, bytes_accessed=moved, transcendentals=0),
    )


def turn_axis(array, axis, start):
    size = array.shape[axis]
    return lax.dynamic_slice_in_dim(jnp.concatenate([array, array], axis), start, size, axis)


def around(array, stride, distance):
    if distance == 0:
        return array
    route = []
    for i in range(lax.axis_size("dp")):
        place = i // stride % RING
        route.append((i, i + ((place + distance) % RING - place) * stride))
    return lax.ppermute(array, "dp", route)


def rounded_sum(*terms):
    return sum(term.astype(jnp.float32) for term in terms).astype(jnp.bfloat16)


def swapped(array):
    return lax.ppermute(array, "section", PAIR)


def per_device(tokens, blocks_in, blocks_out, pos_in, pos_out, cotangent):
    here = lax.axis_index("section")
    owners = lax.axis_size("dp")
    slots = blocks_in.shape[1]
    rows = tokens.shape[0] // 2
    odd = here % 2
    swap = jnp.stack([odd, here // 2]).astype(jnp.int32)
    half = jnp.where((here == 1) | (here == 2), rows, 0)

    own = jnp.stack([blocks_in[0], blocks_out[0]])
    weights = lax.all_gather(jnp.stack([own, swapped(own)]), "dp", axis=0)
    own_places = jnp.stack([pos_in[0], pos_out[0]])
    places = lax.all_gather(jnp.stack([own_places, swapped(own_places)]), "dp", axis=0).transpose(1, 2, 0, 3)
    codes = jnp.arange(owners, dtype=jnp.int32)[:, None] * 8 + jnp.arange(slots, dtype=jnp.int32)
    named = places[..., None] == jnp.arange(NBLK, dtype=jnp.int32)
    where = jnp.max(jnp.where(named, codes[..., None], -1), axis=(2, 3)).reshape(-1)
    where = jnp.where(where < 0, owners * 8, where)
    me = lax.axis_index("dp")
    mine = places[0].reshape(2, RING, RING, 2, slots)
    mine = turn_axis(mine, 1, me // Z)
    mine = turn_axis(mine, 2, (me // Y) % RING)
    mine = turn_axis(mine, 3, me % Y)
    places_in = mine[0].transpose(2, 1, 0, 3).reshape(-1)
    places_out = mine[1].transpose(2, 0, 1, 3).reshape(-1)

    first_tokens = lax.dynamic_slice_in_dim(tokens, half, rows, 0)
    last_grads = lax.dynamic_slice_in_dim(cotangent, half, rows, 0)

    def shape(*dims, dtype=jnp.bfloat16):
        return jax.ShapeDtypeStruct(dims, dtype)

    moved = weights.size * 2
    work = 2 * rows * D * RANK
    anywhere = pl.BlockSpec(memory_space=pl.ANY)

    def held(count):
        return [
            pltpu.VMEM((count, owners + 1, slots, BLOCK, BLOCK), jnp.bfloat16),
            pltpu.SemaphoreType.DMA((count,)),
        ]

    forward = pl.pallas_call(
        forward_kernel,
        out_shape=shape(rows, D),
        grid_spec=pltpu.PrefetchScalarGridSpec(
            num_scalar_prefetch=2,
            grid=(1,),
            in_specs=[whole(rows, D), anywhere],
            out_specs=whole(rows, D),
            scratch_shapes=[pltpu.VMEM((rows, D), jnp.bfloat16), pltpu.VMEM((rows, D), jnp.bfloat16)] + held(4),
        ),
        name="forward_layers",
        **params(4 * work, moved),
    )
    turn = pl.pallas_call(
        turn_kernel,
        out_shape=(
            shape(rows, D),
            shape(2, rows, RANK, dtype=jnp.float32),
            shape(2, rows, BLOCK, dtype=jnp.float32),
            shape(2, rows, D),
            shape(2, rows, RANK),
            shape(rows, D),
        ),
        grid_spec=pltpu.PrefetchScalarGridSpec(
            num_scalar_prefetch=2,
            grid=(1,),
            in_specs=[whole(rows, D)] * 3 + [anywhere],
            out_specs=[
                whole(rows, D),
                whole(2, rows, RANK),
                whole(2, rows, BLOCK),
                whole(2, rows, D),
                whole(2, rows, RANK),
                whole(rows, D),
            ],
            scratch_shapes=[pltpu.VMEM((rows, D), jnp.bfloat16)] * 2 + held(4),
        ),
        name="turn_layers",
        **params(7 * work, moved),
    )

    high = pl.pallas_call(
        high_kernel,
        out_shape=(shape(rows, RANK), shape(rows, D), shape(rows, D), shape(rows // 2, D), shape(rows // 2, D)),
        grid_spec=pltpu.PrefetchScalarGridSpec(
            num_scalar_prefetch=2,
            grid=(1,),
            in_specs=[whole(rows, D)] * 3 + [whole(2, rows, RANK), whole(2, rows, BLOCK), anywhere],
            out_specs=[whole(rows, RANK)] + [whole(rows, D)] * 2 + [whole(rows // 2, D)] * 2,
            scratch_shapes=[pltpu.VMEM((rows, D), jnp.bfloat16)] + held(2),
        ),
        name="backward_high",
        **params(2 * work, moved // 2),
    )
    low = pl.pallas_call(
        low_kernel,
        out_shape=(shape(rows, RANK), shape(rows, RANK)),
        grid_spec=pltpu.PrefetchScalarGridSpec(
            num_scalar_prefetch=2,
            grid=(1,),
            in_specs=[whole(rows, D), whole(rows, RANK), whole(2, rows, RANK), anywhere],
            out_specs=[whole(rows, RANK)] * 2,
            scratch_shapes=held(1),
        ),
        name="backward_low",
        **params(0, 0),
    )

    halves = shape(RING, RING, slots, BLOCK, BLOCK)
    half_spec = pl.BlockSpec((1, RING, slots, BLOCK, BLOCK), lambda step, _: (step, 0, 0, 0, 0))
    dense = pltpu.VMEM((NBLK + 1, BLOCK, BLOCK), jnp.bfloat16)

    def gradient(kernel, name, in_specs, scratch):
        return pl.pallas_call(
            kernel,
            out_shape=(halves, halves),
            grid_spec=pltpu.PrefetchScalarGridSpec(
                num_scalar_prefetch=1,
                grid=(RING,),
                in_specs=in_specs,
                out_specs=(half_spec, half_spec),
                scratch_shapes=[dense] + scratch,
            ),
            name=name,
            **params(0, 0),
        )

    gradient_in = gradient(
        gradient_in_kernel, "gradient_in", [whole(rows, D)] * 2 + [whole(rows, RANK)] * 2, []
    )
    gradient_out = gradient(
        gradient_out_kernel,
        "gradient_out",
        [whole(rows, RANK)] * 2 + [whole(rows, D)] + [whole(rows // 2, D)] * 2,
        [pltpu.VMEM((RANK, 2 * rows), jnp.bfloat16)],
    )
    def core_sums(keep, send):
        arrived = lax.ppermute(send, "dp", CORES)
        return [rounded_sum(keep[i], arrived[i]) for i in range(RING)]

    def scattered(pieces, near, far):
        terms = [around(piece, near, distance) for distance, piece in enumerate(pieces)]
        pieces = [rounded_sum(*[term[i] for term in terms]) for i in range(RING)]
        return rounded_sum(*[around(piece, far, distance) for distance, piece in enumerate(pieces)])[None]

    arrived = lax.ppermute(forward(swap, where, first_tokens, weights), "section", UP)
    second, pre, inverse, normed, act, leaving = turn(swap, where, first_tokens, arrived, last_grads, weights)
    arrived = lax.ppermute(leaving, "section", DOWN)
    arrived, normed_other, act_other = lax.optimization_barrier((arrived, swapped(normed[1]), swapped(act[1])))

    dpre_high, middle, grads_own, early, late = high(swap, where, second, last_grads, arrived, pre, inverse, weights)
    early = swapped(early)
    dpre_own, dpre_sent = low(swap, where, middle, dpre_high, pre, weights)
    early, late, dpre_sent = lax.optimization_barrier((early, late, dpre_sent))
    dpre_other = swapped(dpre_sent)
    late = swapped(late)

    pieces_in = core_sums(*gradient_in(places_in, normed[0], normed_other, dpre_own, dpre_other))
    late, *pieces_in = lax.optimization_barrier((late, *pieces_in))
    pieces_out = core_sums(*gradient_out(places_out, act[0], act_other, grads_own, early, late))
    sums_in = scattered(pieces_in, Y, Z)
    sums_out = scattered(pieces_out, Z, Y)
    return (sums_in, sums_out)


def solution(mesh):
    in_specs = (
        P("dp", None),
        P("section", "dp", None, None),
        P("section", "dp", None, None),
        P("section", "dp"),
        P("section", "dp"),
        P("dp", None),
    )
    out_specs = (P("section", "dp", None, None), P("section", "dp", None, None))
    return jax.shard_map(
        per_device, mesh=mesh, in_specs=in_specs, out_specs=out_specs, check_vma=False
    )
```

```python
import functools

import jax
import jax.numpy as jnp
from jax import lax
from jax.experimental import pallas as pl
from jax.experimental.pallas import tpu as pltpu
from jax.sharding import PartitionSpec as P

D = 8192
RANK = 512
BLOCK = 128
ROWS_D = D // BLOCK
ROWS_K = RANK // BLOCK
NBLK = ROWS_D * ROWS_K
EPS = 1e-05
CHUNK = 1024
BLOCKS = CHUNK // BLOCK
NT = (((1,), (1,)), ((), ()))
NN = (((1,), (0,)), ((), ()))
TN = (((0,), (0,)), ((), ()))
PAIR = [(0, 1), (1, 0), (2, 3), (3, 2)]
UP = [(0, 3), (1, 2)]
DOWN = [(3, 0), (2, 1)]
RING = 4
Y = 2
Z = 8
CORES = [(i, i ^ 1) for i in range(Z * RING)]


def dot(left, right, dims):
    return lax.dot_general(left, right, dims, preferred_element_type=jnp.float32)


class Weights:
    def __init__(self, swap_ref, where_ref, source, held, sems, wanted):
        self.where_ref = where_ref
        self.swap = swap_ref[0]
        self.held = held
        self.order = wanted
        owners = source.shape[0]
        self.copies = {}
        for i, (layer, matrix) in enumerate(wanted):
            copy = pltpu.make_async_copy(source.at[:, layer ^ self.swap, matrix], held.at[i, pl.ds(0, owners)], sems.at[i])
            copy.start()
            self.copies[layer, matrix] = copy
        for i in range(len(wanted)):
            held[i, owners, 0] = jnp.zeros(held.shape[3:], held.dtype)

    def wait(self, layer, matrix):
        self.copies[layer, matrix].wait()

    def block(self, layer, matrix, number):
        code = self.where_ref[((layer ^ self.swap) * 2 + matrix) * NBLK + number]
        return self.held[self.order.index((layer, matrix)), code >> 3, code & 7]

    def rows_in(self, layer, chunk):
        rows = range(chunk * BLOCKS, (chunk + 1) * BLOCKS)
        return jnp.concatenate(
            [
                jnp.concatenate([self.block(layer, 0, row * ROWS_K + col) for col in range(ROWS_K)], axis=1)
                for row in rows
            ],
            axis=0,
        )

    def columns_out(self, layer, chunk):
        cols = range(chunk * BLOCKS, (chunk + 1) * BLOCKS)
        return jnp.concatenate(
            [
                jnp.concatenate([self.block(layer, 1, row * ROWS_D + col) for col in cols], axis=1)
                for row in range(ROWS_K)
            ],
            axis=0,
        )


def chunks():
    return [(chunk, slice(chunk * CHUNK, (chunk + 1) * CHUNK)) for chunk in range(D // CHUNK)]


def forward_down(weights, layer, hidden_ref, normed_ref):
    total = 0.0
    for _, cols in chunks():
        wide = hidden_ref[:, cols].astype(jnp.float32)
        total = total + jnp.sum(wide * wide, axis=-1, keepdims=True)
    inverse = 1.0 / jnp.sqrt(total / D + EPS)
    for _, cols in chunks():
        normed_ref[:, cols] = (hidden_ref[:, cols].astype(jnp.float32) * inverse).astype(jnp.bfloat16)
    weights.wait(layer, 0)
    pre = 0.0
    for chunk, cols in chunks():
        pre = pre + dot(normed_ref[:, cols], weights.rows_in(layer, chunk), NN)
    return pre, inverse


def forward_up(weights, layer, hidden_ref, act, next_ref):
    weights.wait(layer, 1)
    for chunk, cols in chunks():
        moved = dot(act, weights.columns_out(layer, chunk), NN)
        next_ref[:, cols] = (hidden_ref[:, cols].astype(jnp.float32) + moved).astype(jnp.bfloat16)


def backward(weights, layer, hidden_ref, upstream_ref, pre, inverse, earlier_ref):
    dact = 0.0
    for chunk, cols in chunks():
        dact = dact + dot(upstream_ref[:, cols], weights.columns_out(layer, chunk), NT)
    sig = jax.nn.sigmoid(pre)
    dpre = (dact * sig * (1.0 + pre * (1.0 - sig))).astype(jnp.bfloat16)
    if earlier_ref is not None:
        mean = jnp.sum(dpre.astype(jnp.float32) * pre, axis=-1, keepdims=True) / D
        pull = mean * inverse * inverse
        for chunk, cols in chunks():
            dnorm = dot(dpre, weights.rows_in(layer, chunk), NT)
            hidden = hidden_ref[:, cols].astype(jnp.float32)
            earlier_ref[:, cols] = (
                upstream_ref[:, cols].astype(jnp.float32) + dnorm * inverse - hidden * pull
            ).astype(jnp.bfloat16)
    return dpre


def silu(pre):
    return (pre * jax.nn.sigmoid(pre)).astype(jnp.bfloat16)


def forward_kernel(swap_ref, where_ref, first_ref, source, last_ref, second_ref, normed_ref, held, sems):
    weights = Weights(swap_ref, where_ref, source, held, sems, [(0, 0), (0, 1), (1, 0), (1, 1)])
    pre, _ = forward_down(weights, 0, first_ref, normed_ref)
    forward_up(weights, 0, first_ref, silu(pre), second_ref)
    pre, _ = forward_down(weights, 1, second_ref, normed_ref)
    forward_up(weights, 1, second_ref, silu(pre), last_ref)


def choose(arrived, arrived_ref, here_ref, out_ref, sem):
    @pl.when(arrived)
    def _():
        copy = pltpu.make_async_copy(arrived_ref, out_ref, sem)
        copy.start()
        copy.wait()

    @pl.when(jnp.logical_not(arrived))
    def _():
        out_ref[...] = here_ref[...]


def turn_kernel(
    swap_ref, where_ref, tokens_ref, arrived_ref, grad_ref, source, second_ref, pre_ref, inverse_ref, normed_ref, act_ref, earlier_ref, first_ref, middle_ref, held, sems
):
    weights = Weights(swap_ref, where_ref, source, held, sems, [(0, 0), (0, 1), (1, 0), (1, 1)])
    choose(swap_ref[1] > 0, arrived_ref, tokens_ref, first_ref, sems.at[4])
    for layer, hidden_ref in enumerate((first_ref, second_ref)):
        place = layer ^ swap_ref[0]
        pre, inverse = forward_down(weights, layer, hidden_ref, normed_ref.at[place])
        act = silu(pre)
        pre_ref[layer] = pre
        inverse_ref[layer] = jnp.broadcast_to(inverse, inverse_ref.shape[1:])
        act_ref[place] = act
        if layer == 0:
            forward_up(weights, 0, first_ref, act, second_ref)
    weights.wait(1, 1)
    backward(weights, 1, second_ref, grad_ref, pre_ref[1], inverse_ref[1][:, :1], middle_ref)
    backward(weights, 0, first_ref, middle_ref, pre_ref[0], inverse_ref[0][:, :1], earlier_ref)


def high_kernel(
    swap_ref, where_ref, hidden_ref, grad_ref, arrived_ref, pre_ref, inverse_ref, source, dpre_ref, middle_ref, own_ref, sent_ref, upstream_ref, held, sems
):
    weights = Weights(swap_ref, where_ref, source, held, sems, [(1, 1), (1, 0)])
    even = swap_ref[0] == 0
    choose(swap_ref[1] == 0, arrived_ref, grad_ref, upstream_ref, sems.at[2])
    weights.wait(1, 1)
    weights.wait(1, 0)
    dpre_ref[...] = backward(weights, 1, hidden_ref, upstream_ref, pre_ref[1], inverse_ref[1][:, :1], middle_ref)
    for _, cols in chunks():
        upper, lower = upstream_ref[:, cols], middle_ref[:, cols]
        own_ref[:, cols] = lax.select(even, lower, upper)
        sent_ref[:, cols] = lax.select(even, upper, lower)


def low_kernel(swap_ref, where_ref, middle_ref, high_ref, pre_ref, source, own_ref, sent_ref, held, sems):
    weights = Weights(swap_ref, where_ref, source, held, sems, [(0, 1)])
    even = swap_ref[0] == 0
    weights.wait(0, 1)
    low = backward(weights, 0, None, middle_ref, pre_ref[0], None, None)
    high = high_ref[...]
    own_ref[...] = lax.select(even, low, high)
    sent_ref[...] = lax.select(even, high, low)


def pick(places_ref, dense, keep_ref, send_ref):
    step = pl.program_id(0)
    pieces, slots = keep_ref.shape[1], keep_ref.shape[2]
    count = places_ref.shape[0] // 2
    for half, out_ref in enumerate((keep_ref, send_ref)):
        for piece in range(pieces):
            for slot in range(slots):
                index = half * count + step * pieces * slots + piece * slots + slot
                out_ref[0, piece, slot] = dense[places_ref[index]]


def gradient_in_kernel(places_ref, own_ref, other_ref, dpre_own_ref, dpre_other_ref, keep_ref, send_ref, dense):
    @pl.when(pl.program_id(0) == 0)
    def _():
        dense[NBLK] = jnp.zeros((BLOCK, BLOCK), jnp.bfloat16)
        dpre = jnp.concatenate([dpre_own_ref[...], dpre_other_ref[...]], axis=0)
        for chunk, cols in chunks():
            normed = jnp.concatenate([own_ref[:, cols], other_ref[:, cols]], axis=0)
            part = dot(normed, dpre, TN).astype(jnp.bfloat16)
            for row in range(BLOCKS):
                for col in range(ROWS_K):
                    dense[(chunk * BLOCKS + row) * ROWS_K + col] = part[
                        row * BLOCK : (row + 1) * BLOCK, col * BLOCK : (col + 1) * BLOCK
                    ]

    pick(places_ref, dense, keep_ref, send_ref)


def gradient_out_kernel(
    places_ref, act_own_ref, act_other_ref, own_ref, other_ref, keep_ref, send_ref, dense, turned
):
    @pl.when(pl.program_id(0) == 0)
    def _():
        dense[NBLK] = jnp.zeros((BLOCK, BLOCK), jnp.bfloat16)
        act = jnp.concatenate([act_own_ref[...], act_other_ref[...]], axis=0)
        turned[...] = act.astype(jnp.float32).T.astype(jnp.bfloat16)
        for chunk, cols in chunks():
            upstream = jnp.concatenate([own_ref[:, cols], other_ref[:, cols]], axis=0)
            part = dot(turned[...], upstream, NN).astype(jnp.bfloat16)
            for row in range(ROWS_K):
                for col in range(BLOCKS):
                    dense[row * ROWS_D + chunk * BLOCKS + col] = part[
                        row * BLOCK : (row + 1) * BLOCK, col * BLOCK : (col + 1) * BLOCK
                    ]

    pick(places_ref, dense, keep_ref, send_ref)


def whole(*shape):
    return pl.BlockSpec(shape, lambda step, *_: (0,) * len(shape))


def params(flops, moved):
    return dict(
        compiler_params=pltpu.CompilerParams(
            dimension_semantics=("arbitrary",), vmem_limit_bytes=56 * 1024 * 1024
        ),
        cost_estimate=pl.CostEstimate(flops=flops, bytes_accessed=moved, transcendentals=0),
    )


def turn_axis(array, axis, start):
    size = array.shape[axis]
    return lax.dynamic_slice_in_dim(jnp.concatenate([array, array], axis), start, size, axis)


def around(array, stride, distance):
    if distance == 0:
        return array
    route = []
    for i in range(lax.axis_size("dp")):
        place = i // stride % RING
        route.append((i, i + ((place + distance) % RING - place) * stride))
    return lax.ppermute(array, "dp", route)


def rounded_sum(*terms):
    return sum(term.astype(jnp.float32) for term in terms).astype(jnp.bfloat16)


def swapped(array):
    return lax.ppermute(array, "section", PAIR)


def per_device(tokens, blocks_in, blocks_out, pos_in, pos_out, cotangent):
    here = lax.axis_index("section")
    owners = lax.axis_size("dp")
    slots = blocks_in.shape[1]
    rows = tokens.shape[0] // 2
    odd = here % 2
    swap = jnp.stack([odd, here // 2]).astype(jnp.int32)
    half = jnp.where((here == 1) | (here == 2), rows, 0)

    both = jnp.stack([blocks_in[0], blocks_out[0], swapped(blocks_in[0]), swapped(blocks_out[0])])
    weights = lax.all_gather(both, "dp", axis=0).reshape(owners, 2, 2, slots, BLOCK, BLOCK)
    own_places = jnp.stack([pos_in[0], pos_out[0]])
    places = lax.all_gather(jnp.stack([own_places, swapped(own_places)]), "dp", axis=0).transpose(1, 2, 0, 3)
    codes = jnp.arange(owners, dtype=jnp.int32)[:, None] * 8 + jnp.arange(slots, dtype=jnp.int32)
    named = places[..., None] == jnp.arange(NBLK, dtype=jnp.int32)
    where = jnp.max(jnp.where(named, codes[..., None], -1), axis=(2, 3)).reshape(-1)
    where = jnp.where(where < 0, owners * 8, where)
    me = lax.axis_index("dp")
    mine = places[0].reshape(2, RING, RING, 2, slots)
    mine = turn_axis(mine, 1, me // Z)
    mine = turn_axis(mine, 2, (me // Y) % RING)
    mine = turn_axis(mine, 3, me % Y)
    places_in = mine[0].transpose(2, 1, 0, 3).reshape(-1)
    places_out = mine[1].transpose(2, 0, 1, 3).reshape(-1)

    first_tokens = lax.dynamic_slice_in_dim(tokens, half, rows, 0)
    last_grads = lax.dynamic_slice_in_dim(cotangent, half, rows, 0)

    def shape(*dims, dtype=jnp.bfloat16):
        return jax.ShapeDtypeStruct(dims, dtype)

    moved = weights.size * 2
    work = 2 * rows * D * RANK
    anywhere = pl.BlockSpec(memory_space=pl.ANY)

    def held(count):
        return [
            pltpu.VMEM((count, owners + 1, slots, BLOCK, BLOCK), jnp.bfloat16),
            pltpu.SemaphoreType.DMA((count + 1,)),
        ]

    forward = pl.pallas_call(
        forward_kernel,
        out_shape=shape(rows, D),
        grid_spec=pltpu.PrefetchScalarGridSpec(
            num_scalar_prefetch=2,
            grid=(1,),
            in_specs=[whole(rows, D), anywhere],
            out_specs=whole(rows, D),
            scratch_shapes=[pltpu.VMEM((rows, D), jnp.bfloat16), pltpu.VMEM((rows, D), jnp.bfloat16)] + held(4),
        ),
        name="forward_layers",
        **params(4 * work, moved),
    )
    turn = pl.pallas_call(
        turn_kernel,
        out_shape=(
            shape(rows, D),
            shape(2, rows, RANK, dtype=jnp.float32),
            shape(2, rows, BLOCK, dtype=jnp.float32),
            shape(2, rows, D),
            shape(2, rows, RANK),
            shape(rows, D),
        ),
        grid_spec=pltpu.PrefetchScalarGridSpec(
            num_scalar_prefetch=2,
            grid=(1,),
            in_specs=[whole(rows, D), anywhere, whole(rows, D), anywhere],
            out_specs=[
                whole(rows, D),
                whole(2, rows, RANK),
                whole(2, rows, BLOCK),
                whole(2, rows, D),
                whole(2, rows, RANK),
                whole(rows, D),
            ],
            scratch_shapes=[pltpu.VMEM((rows, D), jnp.bfloat16)] * 2 + held(4),
        ),
        name="turn_layers",
        **params(7 * work, moved),
    )

    high = pl.pallas_call(
        high_kernel,
        out_shape=(shape(rows, RANK),) + (shape(rows, D),) * 3,
        grid_spec=pltpu.PrefetchScalarGridSpec(
            num_scalar_prefetch=2,
            grid=(1,),
            in_specs=[whole(rows, D)] * 2 + [anywhere, whole(2, rows, RANK), whole(2, rows, BLOCK), anywhere],
            out_specs=[whole(rows, RANK)] + [whole(rows, D)] * 3,
            scratch_shapes=[pltpu.VMEM((rows, D), jnp.bfloat16)] + held(2),
        ),
        name="backward_high",
        **params(2 * work, moved // 2),
    )
    low = pl.pallas_call(
        low_kernel,
        out_shape=(shape(rows, RANK), shape(rows, RANK)),
        grid_spec=pltpu.PrefetchScalarGridSpec(
            num_scalar_prefetch=2,
            grid=(1,),
            in_specs=[whole(rows, D), whole(rows, RANK), whole(2, rows, RANK), anywhere],
            out_specs=[whole(rows, RANK)] * 2,
            scratch_shapes=held(1),
        ),
        name="backward_low",
        **params(work, moved),
    )

    halves = shape(RING, RING, slots, BLOCK, BLOCK)
    half_spec = pl.BlockSpec((1, RING, slots, BLOCK, BLOCK), lambda step, _: (step, 0, 0, 0, 0))
    dense = pltpu.VMEM((NBLK + 1, BLOCK, BLOCK), jnp.bfloat16)

    def gradient(kernel, name, in_specs, scratch):
        return pl.pallas_call(
            kernel,
            out_shape=(halves, halves),
            grid_spec=pltpu.PrefetchScalarGridSpec(
                num_scalar_prefetch=1,
                grid=(RING,),
                in_specs=in_specs,
                out_specs=(half_spec, half_spec),
                scratch_shapes=[dense] + scratch,
            ),
            name=name,
            **params(2 * work, 3 * moved),
        )

    gradient_in = gradient(
        gradient_in_kernel, "gradient_in", [whole(rows, D)] * 2 + [whole(rows, RANK)] * 2, []
    )
    gradient_out = gradient(
        gradient_out_kernel,
        "gradient_out",
        [whole(rows, RANK)] * 2 + [whole(rows, D)] * 2,
        [pltpu.VMEM((RANK, 2 * rows), jnp.bfloat16)],
    )
    def core_sums(keep, send):
        arrived = lax.ppermute(send, "dp", CORES)
        return [rounded_sum(keep[i], arrived[i]) for i in range(RING)]

    def scattered(pieces, near, far):
        terms = [around(piece, near, distance) for distance, piece in enumerate(pieces)]
        pieces = [rounded_sum(*[term[i] for term in terms]) for i in range(RING)]
        return rounded_sum(*[around(piece, far, distance) for distance, piece in enumerate(pieces)])[None]

    arrived = lax.ppermute(forward(swap, where, first_tokens, weights), "section", UP)
    second, pre, inverse, normed, act, leaving = turn(swap, where, first_tokens, arrived, last_grads, weights)
    arrived = lax.ppermute(leaving, "section", DOWN)
    arrived, normed_other, act_other = lax.optimization_barrier((arrived, swapped(normed[1]), swapped(act[1])))

    dpre_high, middle, grads_own, sent = high(swap, where, second, last_grads, arrived, pre, inverse, weights)
    grads_other = swapped(sent)
    dpre_own, dpre_sent = low(swap, where, middle, dpre_high, pre, weights)
    grads_other, dpre_other = lax.optimization_barrier((grads_other, swapped(dpre_sent)))

    halves_in = gradient_in(places_in, normed[0], normed_other, dpre_own, dpre_other)
    halves_out = gradient_out(places_out, act[0], act_other, grads_own, grads_other)
    pieces_in, pieces_out = core_sums(*halves_in), core_sums(*halves_out)
    sums_in = scattered(pieces_in, Y, Z)
    sums_out = scattered(pieces_out, Z, Y)
    return (sums_in, sums_out)


def solution(mesh):
    in_specs = (
        P("dp", None),
        P("section", "dp", None, None),
        P("section", "dp", None, None),
        P("section", "dp"),
        P("section", "dp"),
        P("dp", None),
    )
    out_specs = (P("section", "dp", None, None), P("section", "dp", None, None))
    return jax.shard_map(
        per_device, mesh=mesh, in_specs=in_specs, out_specs=out_specs, check_vma=False
    )
```

```python
import functools

import jax
import jax.numpy as jnp
from jax import lax
from jax.experimental import pallas as pl
from jax.experimental.pallas import tpu as pltpu
from jax.sharding import PartitionSpec as P

D = 8192
RANK = 512
BLOCK = 128
ROWS_D = D // BLOCK
ROWS_K = RANK // BLOCK
NBLK = ROWS_D * ROWS_K
EPS = 1e-05
CHUNK = 1024
BLOCKS = CHUNK // BLOCK
NT = (((1,), (1,)), ((), ()))
NN = (((1,), (0,)), ((), ()))
TN = (((0,), (0,)), ((), ()))
PAIR = [(0, 1), (1, 0), (2, 3), (3, 2)]
UP = [(0, 3), (1, 2)]
DOWN = [(3, 0), (2, 1)]
RING = 4
Y = 2
Z = 8
NEAR = ((0, 3, 1, 2), (0, 1, 3, 2))
FAR = ((0, 3), (1, 2))
CORES = [(i, i ^ 1) for i in range(Z * RING)]


def dot(left, right, dims):
    return lax.dot_general(left, right, dims, preferred_element_type=jnp.float32)


class Weights:
    def __init__(self, swap_ref, where_ref, source, held, sems, wanted):
        self.where_ref = where_ref
        self.swap = swap_ref[0]
        self.held = held
        self.order = wanted
        owners = source.shape[0]
        self.copies = {}
        for i, (layer, matrix) in enumerate(wanted):
            copy = pltpu.make_async_copy(source.at[:, layer ^ self.swap, matrix], held.at[i, pl.ds(0, owners)], sems.at[i])
            copy.start()
            self.copies[layer, matrix] = copy
        for i in range(len(wanted)):
            held[i, owners, 0] = jnp.zeros(held.shape[3:], held.dtype)

    def wait(self, layer, matrix):
        self.copies[layer, matrix].wait()

    def block(self, layer, matrix, number):
        code = self.where_ref[((layer ^ self.swap) * 2 + matrix) * NBLK + number]
        return self.held[self.order.index((layer, matrix)), code >> 3, code & 7]

    def rows_in(self, layer, chunk):
        rows = range(chunk * BLOCKS, (chunk + 1) * BLOCKS)
        return jnp.concatenate(
            [
                jnp.concatenate([self.block(layer, 0, row * ROWS_K + col) for col in range(ROWS_K)], axis=1)
                for row in rows
            ],
            axis=0,
        )

    def columns_out(self, layer, chunk):
        cols = range(chunk * BLOCKS, (chunk + 1) * BLOCKS)
        return jnp.concatenate(
            [
                jnp.concatenate([self.block(layer, 1, row * ROWS_D + col) for col in cols], axis=1)
                for row in range(ROWS_K)
            ],
            axis=0,
        )


def chunks():
    return [(chunk, slice(chunk * CHUNK, (chunk + 1) * CHUNK)) for chunk in range(D // CHUNK)]


def forward_down(weights, layer, hidden_ref, normed_ref):
    total = 0.0
    for _, cols in chunks():
        wide = hidden_ref[:, cols].astype(jnp.float32)
        total = total + jnp.sum(wide * wide, axis=-1, keepdims=True)
    inverse = 1.0 / jnp.sqrt(total / D + EPS)
    for _, cols in chunks():
        normed_ref[:, cols] = (hidden_ref[:, cols].astype(jnp.float32) * inverse).astype(jnp.bfloat16)
    weights.wait(layer, 0)
    pre = 0.0
    for chunk, cols in chunks():
        pre = pre + dot(normed_ref[:, cols], weights.rows_in(layer, chunk), NN)
    return pre, inverse


def forward_up(weights, layer, hidden_ref, act, next_ref):
    weights.wait(layer, 1)
    for chunk, cols in chunks():
        moved = dot(act, weights.columns_out(layer, chunk), NN)
        next_ref[:, cols] = (hidden_ref[:, cols].astype(jnp.float32) + moved).astype(jnp.bfloat16)


def backward(weights, layer, hidden_ref, upstream_ref, pre, inverse, earlier_ref):
    dact = 0.0
    for chunk, cols in chunks():
        dact = dact + dot(upstream_ref[:, cols], weights.columns_out(layer, chunk), NT)
    sig = jax.nn.sigmoid(pre)
    dpre = (dact * sig * (1.0 + pre * (1.0 - sig))).astype(jnp.bfloat16)
    if earlier_ref is not None:
        mean = jnp.sum(dpre.astype(jnp.float32) * pre, axis=-1, keepdims=True) / D
        pull = mean * inverse * inverse
        for chunk, cols in chunks():
            dnorm = dot(dpre, weights.rows_in(layer, chunk), NT)
            hidden = hidden_ref[:, cols].astype(jnp.float32)
            earlier_ref[:, cols] = (
                upstream_ref[:, cols].astype(jnp.float32) + dnorm * inverse - hidden * pull
            ).astype(jnp.bfloat16)
    return dpre


def silu(pre):
    return (pre * jax.nn.sigmoid(pre)).astype(jnp.bfloat16)


def forward_kernel(swap_ref, where_ref, first_ref, source, last_ref, second_ref, normed_ref, held, sems):
    weights = Weights(swap_ref, where_ref, source, held, sems, [(0, 0), (0, 1), (1, 0), (1, 1)])
    pre, _ = forward_down(weights, 0, first_ref, normed_ref)
    forward_up(weights, 0, first_ref, silu(pre), second_ref)
    pre, _ = forward_down(weights, 1, second_ref, normed_ref)
    forward_up(weights, 1, second_ref, silu(pre), last_ref)


def choose(arrived, arrived_ref, here_ref, out_ref, sem):
    @pl.when(arrived)
    def _():
        copy = pltpu.make_async_copy(arrived_ref, out_ref, sem)
        copy.start()
        copy.wait()

    @pl.when(jnp.logical_not(arrived))
    def _():
        out_ref[...] = here_ref[...]


def turn_kernel(
    swap_ref, where_ref, tokens_ref, arrived_ref, grad_ref, source, second_ref, pre_ref, inverse_ref, normed_own_ref, normed_other_ref, act_own_ref, act_other_ref, earlier_ref, first_ref, middle_ref, normed_ref, act_ref, held, sems
):
    weights = Weights(swap_ref, where_ref, source, held, sems, [(0, 0), (0, 1), (1, 0), (1, 1)])
    choose(swap_ref[1] > 0, arrived_ref, tokens_ref, first_ref, sems.at[4])
    for layer, hidden_ref in enumerate((first_ref, second_ref)):
        place = layer ^ swap_ref[0]
        pre, inverse = forward_down(weights, layer, hidden_ref, normed_ref.at[place])
        act = silu(pre)
        pre_ref[layer] = pre
        inverse_ref[layer] = jnp.broadcast_to(inverse, inverse_ref.shape[1:])
        act_ref[place] = act
        if layer == 0:
            forward_up(weights, 0, first_ref, act, second_ref)
    act_own_ref[...], act_other_ref[...] = act_ref[0], act_ref[1]
    for _, cols in chunks():
        normed_own_ref[:, cols] = normed_ref[0, :, cols]
        normed_other_ref[:, cols] = normed_ref[1, :, cols]
    weights.wait(1, 1)
    backward(weights, 1, second_ref, grad_ref, pre_ref[1], inverse_ref[1][:, :1], middle_ref)
    backward(weights, 0, first_ref, middle_ref, pre_ref[0], inverse_ref[0][:, :1], earlier_ref)


def high_kernel(
    swap_ref, where_ref, hidden_ref, grad_ref, arrived_ref, pre_ref, inverse_ref, source, dpre_ref, middle_ref, own_ref, sent_ref, upstream_ref, held, sems
):
    weights = Weights(swap_ref, where_ref, source, held, sems, [(1, 1), (1, 0)])
    even = swap_ref[0] == 0
    choose(swap_ref[1] == 0, arrived_ref, grad_ref, upstream_ref, sems.at[2])
    weights.wait(1, 1)
    weights.wait(1, 0)
    dpre_ref[...] = backward(weights, 1, hidden_ref, upstream_ref, pre_ref[1], inverse_ref[1][:, :1], middle_ref)
    for _, cols in chunks():
        upper, lower = upstream_ref[:, cols], middle_ref[:, cols]
        own_ref[:, cols] = lax.select(even, lower, upper)
        sent_ref[:, cols] = lax.select(even, upper, lower)


def low_kernel(swap_ref, where_ref, middle_ref, high_ref, pre_ref, source, own_ref, sent_ref, held, sems):
    weights = Weights(swap_ref, where_ref, source, held, sems, [(0, 1)])
    even = swap_ref[0] == 0
    weights.wait(0, 1)
    low = backward(weights, 0, None, middle_ref, pre_ref[0], None, None)
    high = high_ref[...]
    own_ref[...] = lax.select(even, low, high)
    sent_ref[...] = lax.select(even, high, low)


def by_step(values):
    step = pl.program_id(0)
    result = values[0]
    for i, value in enumerate(values[1:], 1):
        result = lax.select(step == i, jnp.int32(value), jnp.int32(result))
    return result


def pick(spots_ref, places_ref, strides, dense, keep_ref, send_ref):
    slots = keep_ref.shape[2]
    for which in range(2):
        near = spots_ref[0] ^ by_step([group[step * 2 + which] for group in NEAR for step in range(2)])
        for other in range(2):
            far = spots_ref[1] ^ by_step([group[other] for group in FAR for _ in range(2)])
            for half, out_ref in enumerate((keep_ref, send_ref)):
                owner = near * strides[0] + far * strides[1] + (spots_ref[2] ^ half)
                for slot in range(slots):
                    out_ref[0, which * 2 + other, slot] = dense[places_ref[owner * slots + slot]]


def gradient_in_kernel(spots_ref, places_ref, own_ref, other_ref, dpre_own_ref, dpre_other_ref, keep_ref, send_ref, dense):
    @pl.when(pl.program_id(0) == 0)
    def _():
        dense[NBLK] = jnp.zeros((BLOCK, BLOCK), jnp.bfloat16)
        dpre = jnp.concatenate([dpre_own_ref[...], dpre_other_ref[...]], axis=0)
        for chunk, cols in chunks():
            normed = jnp.concatenate([own_ref[:, cols], other_ref[:, cols]], axis=0)
            part = dot(normed, dpre, TN).astype(jnp.bfloat16)
            for row in range(BLOCKS):
                for col in range(ROWS_K):
                    dense[(chunk * BLOCKS + row) * ROWS_K + col] = part[
                        row * BLOCK : (row + 1) * BLOCK, col * BLOCK : (col + 1) * BLOCK
                    ]

    pick(spots_ref, places_ref, (Y, Z), dense, keep_ref, send_ref)


def gradient_out_kernel(
    spots_ref, places_ref, act_own_ref, act_other_ref, own_ref, other_ref, keep_ref, send_ref, dense, turned
):
    @pl.when(pl.program_id(0) == 0)
    def _():
        dense[NBLK] = jnp.zeros((BLOCK, BLOCK), jnp.bfloat16)
        act = jnp.concatenate([act_own_ref[...], act_other_ref[...]], axis=0)
        turned[...] = act.astype(jnp.float32).T.astype(jnp.bfloat16)
        for chunk, cols in chunks():
            upstream = jnp.concatenate([own_ref[:, cols], other_ref[:, cols]], axis=0)
            part = dot(turned[...], upstream, NN).astype(jnp.bfloat16)
            for row in range(ROWS_K):
                for col in range(BLOCKS):
                    dense[row * ROWS_D + chunk * BLOCKS + col] = part[
                        row * BLOCK : (row + 1) * BLOCK, col * BLOCK : (col + 1) * BLOCK
                    ]

    pick(spots_ref, places_ref, (Z, Y), dense, keep_ref, send_ref)


def whole(*shape):
    return pl.BlockSpec(shape, lambda step, *_: (0,) * len(shape))


def params(flops, moved):
    return dict(
        compiler_params=pltpu.CompilerParams(
            dimension_semantics=("arbitrary",), vmem_limit_bytes=56 * 1024 * 1024
        ),
        cost_estimate=pl.CostEstimate(flops=flops, bytes_accessed=moved, transcendentals=0),
    )


def across(array, stride, flip):
    if flip == 0:
        return array
    devices = range(lax.axis_size("dp"))
    return lax.ppermute(array, "dp", [(i, i + ((i // stride % RING ^ flip) - i // stride % RING) * stride) for i in devices])


def rounded_sum(*terms):
    return sum(term.astype(jnp.float32) for term in terms).astype(jnp.bfloat16)


def swapped(array):
    return lax.ppermute(array, "section", PAIR)


def per_device(tokens, blocks_in, blocks_out, pos_in, pos_out, cotangent):
    here = lax.axis_index("section")
    owners = lax.axis_size("dp")
    slots = blocks_in.shape[1]
    rows = tokens.shape[0] // 2
    odd = here % 2
    swap = jnp.stack([odd, here // 2]).astype(jnp.int32)
    half = jnp.where((here == 1) | (here == 2), rows, 0)

    both = jnp.stack([blocks_in[0], blocks_out[0], swapped(blocks_in[0]), swapped(blocks_out[0])])
    weights = lax.all_gather(both, "dp", axis=0).reshape(owners, 2, 2, slots, BLOCK, BLOCK)
    own_places = jnp.stack([pos_in[0], pos_out[0]])
    places = lax.all_gather(jnp.stack([own_places, swapped(own_places)]), "dp", axis=0).transpose(1, 2, 0, 3)
    codes = jnp.arange(owners, dtype=jnp.int32)[:, None] * 8 + jnp.arange(slots, dtype=jnp.int32)
    named = places[..., None] == jnp.arange(NBLK, dtype=jnp.int32)
    where = jnp.max(jnp.where(named, codes[..., None], -1), axis=(2, 3)).reshape(-1)
    where = jnp.where(where < 0, owners * 8, where)
    places_in, places_out = places[0, 0].reshape(-1), places[0, 1].reshape(-1)
    me = lax.axis_index("dp")
    spot_z, spot_y, spot_core = me // Z, me // Y % RING, me % Y
    spots_in = jnp.stack([spot_y, spot_z, spot_core]).astype(jnp.int32)
    spots_out = jnp.stack([spot_z, spot_y, spot_core]).astype(jnp.int32)

    first_tokens = lax.dynamic_slice_in_dim(tokens, half, rows, 0)
    last_grads = lax.dynamic_slice_in_dim(cotangent, half, rows, 0)

    def shape(*dims, dtype=jnp.bfloat16):
        return jax.ShapeDtypeStruct(dims, dtype)

    moved = weights.size * 2
    work = 2 * rows * D * RANK
    anywhere = pl.BlockSpec(memory_space=pl.ANY)

    def held(count):
        return [
            pltpu.VMEM((count, owners + 1, slots, BLOCK, BLOCK), jnp.bfloat16),
            pltpu.SemaphoreType.DMA((count + 1,)),
        ]

    forward = pl.pallas_call(
        forward_kernel,
        out_shape=shape(rows, D),
        grid_spec=pltpu.PrefetchScalarGridSpec(
            num_scalar_prefetch=2,
            grid=(1,),
            in_specs=[whole(rows, D), anywhere],
            out_specs=whole(rows, D),
            scratch_shapes=[pltpu.VMEM((rows, D), jnp.bfloat16), pltpu.VMEM((rows, D), jnp.bfloat16)] + held(4),
        ),
        name="forward_layers",
        **params(4 * work, moved),
    )
    turn = pl.pallas_call(
        turn_kernel,
        out_shape=(
            shape(rows, D),
            shape(2, rows, RANK, dtype=jnp.float32),
            shape(2, rows, BLOCK, dtype=jnp.float32),
            shape(rows, D),
            shape(rows, D),
            shape(rows, RANK),
            shape(rows, RANK),
            shape(rows, D),
        ),
        grid_spec=pltpu.PrefetchScalarGridSpec(
            num_scalar_prefetch=2,
            grid=(1,),
            in_specs=[whole(rows, D), anywhere, whole(rows, D), anywhere],
            out_specs=[
                whole(rows, D),
                whole(2, rows, RANK),
                whole(2, rows, BLOCK),
                whole(rows, D),
                whole(rows, D),
                whole(rows, RANK),
                whole(rows, RANK),
                whole(rows, D),
            ],
            scratch_shapes=[pltpu.VMEM((rows, D), jnp.bfloat16)] * 2
            + [pltpu.VMEM((2, rows, D), jnp.bfloat16), pltpu.VMEM((2, rows, RANK), jnp.bfloat16)]
            + held(4),
        ),
        name="turn_layers",
        **params(7 * work, moved),
    )

    high = pl.pallas_call(
        high_kernel,
        out_shape=(shape(rows, RANK),) + (shape(rows, D),) * 3,
        grid_spec=pltpu.PrefetchScalarGridSpec(
            num_scalar_prefetch=2,
            grid=(1,),
            in_specs=[whole(rows, D)] * 2 + [anywhere, whole(2, rows, RANK), whole(2, rows, BLOCK), anywhere],
            out_specs=[whole(rows, RANK)] + [whole(rows, D)] * 3,
            scratch_shapes=[pltpu.VMEM((rows, D), jnp.bfloat16)] + held(2),
        ),
        name="backward_high",
        **params(2 * work, moved // 2),
    )
    low = pl.pallas_call(
        low_kernel,
        out_shape=(shape(rows, RANK), shape(rows, RANK)),
        grid_spec=pltpu.PrefetchScalarGridSpec(
            num_scalar_prefetch=2,
            grid=(1,),
            in_specs=[whole(rows, D), whole(rows, RANK), whole(2, rows, RANK), anywhere],
            out_specs=[whole(rows, RANK)] * 2,
            scratch_shapes=held(1),
        ),
        name="backward_low",
        **params(work, moved),
    )

    halves = shape(RING, RING, slots, BLOCK, BLOCK)
    half_spec = pl.BlockSpec((1, RING, slots, BLOCK, BLOCK), lambda step, *_: (step, 0, 0, 0, 0))
    dense = pltpu.VMEM((NBLK + 1, BLOCK, BLOCK), jnp.bfloat16)

    def gradient(kernel, name, in_specs, scratch):
        return pl.pallas_call(
            kernel,
            out_shape=(halves, halves),
            grid_spec=pltpu.PrefetchScalarGridSpec(
                num_scalar_prefetch=2,
                grid=(RING,),
                in_specs=in_specs,
                out_specs=(half_spec, half_spec),
                scratch_shapes=[dense] + scratch,
            ),
            name=name,
            **params(2 * work, 3 * moved),
        )

    gradient_in = gradient(
        gradient_in_kernel, "gradient_in", [whole(rows, D)] * 2 + [whole(rows, RANK)] * 2, []
    )
    gradient_out = gradient(
        gradient_out_kernel,
        "gradient_out",
        [whole(rows, RANK)] * 2 + [whole(rows, D)] * 2,
        [pltpu.VMEM((RANK, 2 * rows), jnp.bfloat16)],
    )
    def core_sums(keep, send):
        arrived = lax.ppermute(send, "dp", CORES)
        return [rounded_sum(keep[i], arrived[i]) for i in range(RING)]

    def scattered(pieces, near, far):
        sums = []
        for kept, sent, (_, second, first, _) in zip(pieces[::2], pieces[1::2], NEAR):
            arrived = across(sent, near, first)
            mine = rounded_sum(kept[:2], arrived[:2])
            arrived = across(rounded_sum(kept[2:], arrived[2:]), near, second)
            sums += [rounded_sum(mine[i], arrived[i]) for i in range(2)]
        return rounded_sum(*[across(term, far, step) for term, step in zip(sums, FAR[0] + FAR[1])])[None]

    arrived = lax.ppermute(forward(swap, where, first_tokens, weights), "section", UP)
    second, pre, inverse, normed_own, normed_sent, act_own, act_sent, leaving = turn(swap, where, first_tokens, arrived, last_grads, weights)
    arrived = lax.ppermute(leaving, "section", DOWN)
    normed_sent, act_other = lax.optimization_barrier((normed_sent, swapped(act_sent)))
    arrived, normed_other = lax.optimization_barrier((arrived, swapped(normed_sent)))

    dpre_high, middle, grads_own, sent = high(swap, where, second, last_grads, arrived, pre, inverse, weights)
    grads_other = swapped(sent)
    dpre_own, dpre_sent = low(swap, where, middle, dpre_high, pre, weights)
    grads_other, dpre_other = lax.optimization_barrier((grads_other, swapped(dpre_sent)))

    halves_in = gradient_in(spots_in, places_in, normed_own, normed_other, dpre_own, dpre_other)
    halves_out = gradient_out(spots_out, places_out, act_own, act_other, grads_own, grads_other)
    pieces_in, pieces_out = core_sums(*halves_in), core_sums(*halves_out)
    sums_in = scattered(pieces_in, Y, Z)
    sums_out = scattered(pieces_out, Z, Y)
    return (sums_in, sums_out)


def solution(mesh):
    in_specs = (
        P("dp", None),
        P("section", "dp", None, None),
        P("section", "dp", None, None),
        P("section", "dp"),
        P("section", "dp"),
        P("dp", None),
    )
    out_specs = (P("section", "dp", None, None), P("section", "dp", None, None))
    return jax.shard_map(
        per_device, mesh=mesh, in_specs=in_specs, out_specs=out_specs, check_vma=False
    )
```

```python
import functools

import jax
import jax.numpy as jnp
from jax import lax
from jax.experimental import pallas as pl
from jax.experimental.pallas import tpu as pltpu
from jax.sharding import PartitionSpec as P

D = 8192
RANK = 512
BLOCK = 128
ROWS_D = D // BLOCK
ROWS_K = RANK // BLOCK
NBLK = ROWS_D * ROWS_K
EPS = 1e-05
CHUNK = 1024
BLOCKS = CHUNK // BLOCK
NT = (((1,), (1,)), ((), ()))
NN = (((1,), (0,)), ((), ()))
TN = (((0,), (0,)), ((), ()))
PAIR = [(0, 1), (1, 0), (2, 3), (3, 2)]
UP = [(0, 3), (1, 2)]
DOWN = [(3, 0), (2, 1)]
RING = 4
Y = 2
Z = 8
NEAR = ((0, 3, 1, 2), (0, 1, 3, 2))
FAR = ((0, 3), (1, 2))
CORES = [(i, i ^ 1) for i in range(Z * RING)]


def dot(left, right, dims):
    return lax.dot_general(left, right, dims, preferred_element_type=jnp.float32)


class Weights:
    def __init__(self, swap_ref, where_ref, source, held, sems, wanted):
        self.where_ref = where_ref
        self.swap = swap_ref[0]
        self.held = held
        self.order = wanted
        owners = source.shape[0]
        self.copies = {}
        for i, (layer, matrix) in enumerate(wanted):
            copy = pltpu.make_async_copy(source.at[:, layer ^ self.swap, matrix], held.at[i, pl.ds(0, owners)], sems.at[i])
            copy.start()
            self.copies[layer, matrix] = copy
        for i in range(len(wanted)):
            held[i, owners, 0] = jnp.zeros(held.shape[3:], held.dtype)

    def wait(self, layer, matrix):
        copy = self.copies.pop((layer, matrix), None)
        if copy is not None:
            copy.wait()

    def block(self, layer, matrix, number):
        code = self.where_ref[((layer ^ self.swap) * 2 + matrix) * NBLK + number]
        return self.held[self.order.index((layer, matrix)), code >> 3, code & 7]

    def rows_in(self, layer, chunk):
        rows = range(chunk * BLOCKS, (chunk + 1) * BLOCKS)
        return jnp.concatenate(
            [
                jnp.concatenate([self.block(layer, 0, row * ROWS_K + col) for col in range(ROWS_K)], axis=1)
                for row in rows
            ],
            axis=0,
        )

    def columns_out(self, layer, chunk):
        cols = range(chunk * BLOCKS, (chunk + 1) * BLOCKS)
        return jnp.concatenate(
            [
                jnp.concatenate([self.block(layer, 1, row * ROWS_D + col) for col in cols], axis=1)
                for row in range(ROWS_K)
            ],
            axis=0,
        )


def chunks():
    return [(chunk, slice(chunk * CHUNK, (chunk + 1) * CHUNK)) for chunk in range(D // CHUNK)]


def forward_down(weights, layer, hidden_ref, normed_ref):
    total = 0.0
    for _, cols in chunks():
        wide = hidden_ref[:, cols].astype(jnp.float32)
        total = total + jnp.sum(wide * wide, axis=-1, keepdims=True)
    inverse = 1.0 / jnp.sqrt(total / D + EPS)
    for _, cols in chunks():
        normed_ref[:, cols] = (hidden_ref[:, cols].astype(jnp.float32) * inverse).astype(jnp.bfloat16)
    weights.wait(layer, 0)
    pre = 0.0
    for chunk, cols in chunks():
        pre = pre + dot(normed_ref[:, cols], weights.rows_in(layer, chunk), NN)
    return pre, inverse


def forward_up(weights, layer, hidden_ref, act, next_ref):
    weights.wait(layer, 1)
    for chunk, cols in chunks():
        moved = dot(act, weights.columns_out(layer, chunk), NN)
        next_ref[:, cols] = (hidden_ref[:, cols].astype(jnp.float32) + moved).astype(jnp.bfloat16)


def backward(weights, layer, hidden_ref, upstream_ref, pre, inverse, earlier_ref):
    weights.wait(layer, 1)
    dact = 0.0
    for chunk, cols in chunks():
        dact = dact + dot(upstream_ref[:, cols], weights.columns_out(layer, chunk), NT)
    sig = jax.nn.sigmoid(pre)
    dpre = (dact * sig * (1.0 + pre * (1.0 - sig))).astype(jnp.bfloat16)
    if earlier_ref is not None:
        mean = jnp.sum(dpre.astype(jnp.float32) * pre, axis=-1, keepdims=True) / D
        pull = mean * inverse * inverse
        weights.wait(layer, 0)
        for chunk, cols in chunks():
            dnorm = dot(dpre, weights.rows_in(layer, chunk), NT)
            hidden = hidden_ref[:, cols].astype(jnp.float32)
            earlier_ref[:, cols] = (
                upstream_ref[:, cols].astype(jnp.float32) + dnorm * inverse - hidden * pull
            ).astype(jnp.bfloat16)
    return dpre


def silu(pre):
    return (pre * jax.nn.sigmoid(pre)).astype(jnp.bfloat16)


def forward_kernel(swap_ref, where_ref, first_ref, source, last_ref, second_ref, normed_ref, held, sems):
    weights = Weights(swap_ref, where_ref, source, held, sems, [(0, 0), (0, 1), (1, 0), (1, 1)])
    pre, _ = forward_down(weights, 0, first_ref, normed_ref)
    forward_up(weights, 0, first_ref, silu(pre), second_ref)
    pre, _ = forward_down(weights, 1, second_ref, normed_ref)
    forward_up(weights, 1, second_ref, silu(pre), last_ref)


class Choice:
    def __init__(self, arrived, arrived_ref, here_ref, out_ref, sem):
        self.arrived = arrived
        self.copy = pltpu.make_async_copy(arrived_ref, out_ref, sem)

        @pl.when(arrived)
        def _():
            self.copy.start()

        @pl.when(jnp.logical_not(arrived))
        def _():
            out_ref[...] = here_ref[...]

    def wait(self):
        @pl.when(self.arrived)
        def _():
            self.copy.wait()


def turn_kernel(
    swap_ref, where_ref, tokens_ref, arrived_ref, grad_ref, source, second_ref, pre_ref, inverse_ref, normed_own_ref, normed_other_ref, act_own_ref, act_other_ref, earlier_ref, first_ref, middle_ref, normed_ref, act_ref, held, sems
):
    choice = Choice(swap_ref[1] > 0, arrived_ref, tokens_ref, first_ref, sems.at[4])
    weights = Weights(swap_ref, where_ref, source, held, sems, [(0, 0), (0, 1), (1, 0), (1, 1)])
    choice.wait()
    for layer, hidden_ref in enumerate((first_ref, second_ref)):
        place = layer ^ swap_ref[0]
        pre, inverse = forward_down(weights, layer, hidden_ref, normed_ref.at[place])
        act = silu(pre)
        pre_ref[layer] = pre
        inverse_ref[layer] = jnp.broadcast_to(inverse, inverse_ref.shape[1:])
        act_ref[place] = act
        if layer == 0:
            forward_up(weights, 0, first_ref, act, second_ref)
    act_own_ref[...], act_other_ref[...] = act_ref[0], act_ref[1]
    for _, cols in chunks():
        normed_own_ref[:, cols] = normed_ref[0, :, cols]
        normed_other_ref[:, cols] = normed_ref[1, :, cols]
    backward(weights, 1, second_ref, grad_ref, pre_ref[1], inverse_ref[1][:, :1], middle_ref)
    backward(weights, 0, first_ref, middle_ref, pre_ref[0], inverse_ref[0][:, :1], earlier_ref)


def high_kernel(
    swap_ref, where_ref, hidden_ref, grad_ref, arrived_ref, pre_ref, inverse_ref, source, dpre_ref, middle_ref, own_ref, sent_ref, upstream_ref, held, sems
):
    choice = Choice(swap_ref[1] == 0, arrived_ref, grad_ref, upstream_ref, sems.at[2])
    weights = Weights(swap_ref, where_ref, source, held, sems, [(1, 1), (1, 0)])
    even = swap_ref[0] == 0
    choice.wait()
    dpre_ref[...] = backward(weights, 1, hidden_ref, upstream_ref, pre_ref[1], inverse_ref[1][:, :1], middle_ref)
    for _, cols in chunks():
        upper, lower = upstream_ref[:, cols], middle_ref[:, cols]
        own_ref[:, cols] = lax.select(even, lower, upper)
        sent_ref[:, cols] = lax.select(even, upper, lower)


def low_kernel(swap_ref, where_ref, middle_ref, high_ref, pre_ref, source, own_ref, sent_ref, held, sems):
    weights = Weights(swap_ref, where_ref, source, held, sems, [(0, 1)])
    even = swap_ref[0] == 0
    low = backward(weights, 0, None, middle_ref, pre_ref[0], None, None)
    high = high_ref[...]
    own_ref[...] = lax.select(even, low, high)
    sent_ref[...] = lax.select(even, high, low)


def by_step(values):
    step = pl.program_id(0)
    result = values[0]
    for i, value in enumerate(values[1:], 1):
        result = lax.select(step == i, jnp.int32(value), jnp.int32(result))
    return result


def pick(spots_ref, places_ref, strides, dense, keep_ref, send_ref):
    slots = keep_ref.shape[2]
    for which in range(2):
        near = spots_ref[0] ^ by_step([group[step * 2 + which] for group in NEAR for step in range(2)])
        for other in range(2):
            far = spots_ref[1] ^ by_step([group[other] for group in FAR for _ in range(2)])
            for half, out_ref in enumerate((keep_ref, send_ref)):
                owner = near * strides[0] + far * strides[1] + (spots_ref[2] ^ half)
                for slot in range(slots):
                    out_ref[0, which * 2 + other, slot] = dense[places_ref[owner * slots + slot]]


def gradient_in_kernel(spots_ref, places_ref, own_ref, other_ref, dpre_own_ref, dpre_other_ref, keep_ref, send_ref, dense):
    @pl.when(pl.program_id(0) == 0)
    def _():
        dense[NBLK] = jnp.zeros((BLOCK, BLOCK), jnp.bfloat16)
        dpre = jnp.concatenate([dpre_own_ref[...], dpre_other_ref[...]], axis=0)
        for chunk, cols in chunks():
            normed = jnp.concatenate([own_ref[:, cols], other_ref[:, cols]], axis=0)
            part = dot(normed, dpre, TN).astype(jnp.bfloat16)
            for row in range(BLOCKS):
                for col in range(ROWS_K):
                    dense[(chunk * BLOCKS + row) * ROWS_K + col] = part[
                        row * BLOCK : (row + 1) * BLOCK, col * BLOCK : (col + 1) * BLOCK
                    ]

    pick(spots_ref, places_ref, (Y, Z), dense, keep_ref, send_ref)


def gradient_out_kernel(
    spots_ref, places_ref, act_own_ref, act_other_ref, own_ref, other_ref, keep_ref, send_ref, dense, turned
):
    @pl.when(pl.program_id(0) == 0)
    def _():
        dense[NBLK] = jnp.zeros((BLOCK, BLOCK), jnp.bfloat16)
        act = jnp.concatenate([act_own_ref[...], act_other_ref[...]], axis=0)
        turned[...] = act.astype(jnp.float32).T.astype(jnp.bfloat16)
        for chunk, cols in chunks():
            upstream = jnp.concatenate([own_ref[:, cols], other_ref[:, cols]], axis=0)
            part = dot(turned[...], upstream, NN).astype(jnp.bfloat16)
            for row in range(ROWS_K):
                for col in range(BLOCKS):
                    dense[row * ROWS_D + chunk * BLOCKS + col] = part[
                        row * BLOCK : (row + 1) * BLOCK, col * BLOCK : (col + 1) * BLOCK
                    ]

    pick(spots_ref, places_ref, (Z, Y), dense, keep_ref, send_ref)


def whole(*shape):
    return pl.BlockSpec(shape, lambda step, *_: (0,) * len(shape))


def params(flops, moved):
    return dict(
        compiler_params=pltpu.CompilerParams(
            dimension_semantics=("arbitrary",), vmem_limit_bytes=56 * 1024 * 1024
        ),
        cost_estimate=pl.CostEstimate(flops=flops, bytes_accessed=moved, transcendentals=0),
    )


def across(array, stride, flip):
    if flip == 0:
        return array
    devices = range(lax.axis_size("dp"))
    return lax.ppermute(array, "dp", [(i, i + ((i // stride % RING ^ flip) - i // stride % RING) * stride) for i in devices])


def rounded_sum(*terms):
    return sum(term.astype(jnp.float32) for term in terms).astype(jnp.bfloat16)


def swapped(array):
    return lax.ppermute(array, "section", PAIR)


def per_device(tokens, blocks_in, blocks_out, pos_in, pos_out, cotangent):
    here = lax.axis_index("section")
    owners = lax.axis_size("dp")
    slots = blocks_in.shape[1]
    rows = tokens.shape[0] // 2
    odd = here % 2
    swap = jnp.stack([odd, here // 2]).astype(jnp.int32)
    half = jnp.where((here == 1) | (here == 2), rows, 0)

    both = jnp.stack([blocks_in[0], blocks_out[0], swapped(blocks_in[0]), swapped(blocks_out[0])])
    weights = lax.all_gather(both, "dp", axis=0).reshape(owners, 2, 2, slots, BLOCK, BLOCK)
    own_places = jnp.stack([pos_in[0], pos_out[0]])
    places = lax.all_gather(jnp.stack([own_places, swapped(own_places)]), "dp", axis=0).transpose(1, 2, 0, 3)
    codes = jnp.arange(owners, dtype=jnp.int32)[:, None] * 8 + jnp.arange(slots, dtype=jnp.int32)
    named = places[..., None] == jnp.arange(NBLK, dtype=jnp.int32)
    where = jnp.max(jnp.where(named, codes[..., None], -1), axis=(2, 3)).reshape(-1)
    where = jnp.where(where < 0, owners * 8, where)
    places_in, places_out = places[0, 0].reshape(-1), places[0, 1].reshape(-1)
    me = lax.axis_index("dp")
    spot_z, spot_y, spot_core = me // Z, me // Y % RING, me % Y
    spots_in = jnp.stack([spot_y, spot_z, spot_core]).astype(jnp.int32)
    spots_out = jnp.stack([spot_z, spot_y, spot_core]).astype(jnp.int32)

    first_tokens = lax.dynamic_slice_in_dim(tokens, half, rows, 0)
    last_grads = lax.dynamic_slice_in_dim(cotangent, half, rows, 0)

    def shape(*dims, dtype=jnp.bfloat16):
        return jax.ShapeDtypeStruct(dims, dtype)

    moved = weights.size * 2
    work = 2 * rows * D * RANK
    anywhere = pl.BlockSpec(memory_space=pl.ANY)

    def held(count):
        return [
            pltpu.VMEM((count, owners + 1, slots, BLOCK, BLOCK), jnp.bfloat16),
            pltpu.SemaphoreType.DMA((count + 1,)),
        ]

    forward = pl.pallas_call(
        forward_kernel,
        out_shape=shape(rows, D),
        grid_spec=pltpu.PrefetchScalarGridSpec(
            num_scalar_prefetch=2,
            grid=(1,),
            in_specs=[whole(rows, D), anywhere],
            out_specs=whole(rows, D),
            scratch_shapes=[pltpu.VMEM((rows, D), jnp.bfloat16), pltpu.VMEM((rows, D), jnp.bfloat16)] + held(4),
        ),
        name="forward_layers",
        **params(4 * work, moved),
    )
    turn = pl.pallas_call(
        turn_kernel,
        out_shape=(
            shape(rows, D),
            shape(2, rows, RANK, dtype=jnp.float32),
            shape(2, rows, BLOCK, dtype=jnp.float32),
            shape(rows, D),
            shape(rows, D),
            shape(rows, RANK),
            shape(rows, RANK),
            shape(rows, D),
        ),
        grid_spec=pltpu.PrefetchScalarGridSpec(
            num_scalar_prefetch=2,
            grid=(1,),
            in_specs=[whole(rows, D), anywhere, whole(rows, D), anywhere],
            out_specs=[
                whole(rows, D),
                whole(2, rows, RANK),
                whole(2, rows, BLOCK),
                whole(rows, D),
                whole(rows, D),
                whole(rows, RANK),
                whole(rows, RANK),
                whole(rows, D),
            ],
            scratch_shapes=[pltpu.VMEM((rows, D), jnp.bfloat16)] * 2
            + [pltpu.VMEM((2, rows, D), jnp.bfloat16), pltpu.VMEM((2, rows, RANK), jnp.bfloat16)]
            + held(4),
        ),
        name="turn_layers",
        **params(7 * work, moved),
    )

    high = pl.pallas_call(
        high_kernel,
        out_shape=(shape(rows, RANK),) + (shape(rows, D),) * 3,
        grid_spec=pltpu.PrefetchScalarGridSpec(
            num_scalar_prefetch=2,
            grid=(1,),
            in_specs=[whole(rows, D)] * 2 + [anywhere, whole(2, rows, RANK), whole(2, rows, BLOCK), anywhere],
            out_specs=[whole(rows, RANK)] + [whole(rows, D)] * 3,
            scratch_shapes=[pltpu.VMEM((rows, D), jnp.bfloat16)] + held(2),
        ),
        name="backward_high",
        **params(2 * work, moved // 2),
    )
    low = pl.pallas_call(
        low_kernel,
        out_shape=(shape(rows, RANK), shape(rows, RANK)),
        grid_spec=pltpu.PrefetchScalarGridSpec(
            num_scalar_prefetch=2,
            grid=(1,),
            in_specs=[whole(rows, D), whole(rows, RANK), whole(2, rows, RANK), anywhere],
            out_specs=[whole(rows, RANK)] * 2,
            scratch_shapes=held(1),
        ),
        name="backward_low",
        **params(work, moved),
    )

    halves = shape(RING, RING, slots, BLOCK, BLOCK)
    half_spec = pl.BlockSpec((1, RING, slots, BLOCK, BLOCK), lambda step, *_: (step, 0, 0, 0, 0))
    dense = pltpu.VMEM((NBLK + 1, BLOCK, BLOCK), jnp.bfloat16)

    def gradient(kernel, name, in_specs, scratch):
        return pl.pallas_call(
            kernel,
            out_shape=(halves, halves),
            grid_spec=pltpu.PrefetchScalarGridSpec(
                num_scalar_prefetch=2,
                grid=(RING,),
                in_specs=in_specs,
                out_specs=(half_spec, half_spec),
                scratch_shapes=[dense] + scratch,
            ),
            name=name,
            **params(2 * work, 3 * moved),
        )

    gradient_in = gradient(
        gradient_in_kernel, "gradient_in", [whole(rows, D)] * 2 + [whole(rows, RANK)] * 2, []
    )
    gradient_out = gradient(
        gradient_out_kernel,
        "gradient_out",
        [whole(rows, RANK)] * 2 + [whole(rows, D)] * 2,
        [pltpu.VMEM((RANK, 2 * rows), jnp.bfloat16)],
    )
    def core_sums(keep, send):
        arrived = lax.ppermute(send, "dp", CORES)
        return [rounded_sum(keep[i], arrived[i]) for i in range(RING)]

    def scattered(pieces, near, far):
        sums = []
        for kept, sent, (_, second, first, _) in zip(pieces[::2], pieces[1::2], NEAR):
            arrived = across(sent, near, first)
            mine = rounded_sum(kept[:2], arrived[:2])
            arrived = across(rounded_sum(kept[2:], arrived[2:]), near, second)
            sums += [rounded_sum(mine[i], arrived[i]) for i in range(2)]
        return rounded_sum(*[across(term, far, step) for term, step in zip(sums, FAR[0] + FAR[1])])[None]

    arrived = lax.ppermute(forward(swap, where, first_tokens, weights), "section", UP)
    second, pre, inverse, normed_own, normed_sent, act_own, act_sent, leaving = turn(swap, where, first_tokens, arrived, last_grads, weights)
    arrived = lax.ppermute(leaving, "section", DOWN)
    normed_sent, act_other = lax.optimization_barrier((normed_sent, swapped(act_sent)))
    arrived, normed_other = lax.optimization_barrier((arrived, swapped(normed_sent)))

    dpre_high, middle, grads_own, sent = high(swap, where, second, last_grads, arrived, pre, inverse, weights)
    grads_other = swapped(sent)
    dpre_own, dpre_sent = low(swap, where, middle, dpre_high, pre, weights)
    grads_other, dpre_other = lax.optimization_barrier((grads_other, swapped(dpre_sent)))

    halves_in = gradient_in(spots_in, places_in, normed_own, normed_other, dpre_own, dpre_other)
    halves_out = gradient_out(spots_out, places_out, act_own, act_other, grads_own, grads_other)
    pieces_in, pieces_out = core_sums(*halves_in), core_sums(*halves_out)
    sums_in = scattered(pieces_in, Y, Z)
    sums_out = scattered(pieces_out, Z, Y)
    return (sums_in, sums_out)


def solution(mesh):
    in_specs = (
        P("dp", None),
        P("section", "dp", None, None),
        P("section", "dp", None, None),
        P("section", "dp"),
        P("section", "dp"),
        P("dp", None),
    )
    out_specs = (P("section", "dp", None, None), P("section", "dp", None, None))
    return jax.shard_map(
        per_device, mesh=mesh, in_specs=in_specs, out_specs=out_specs, check_vma=False
    )
```

```python
import functools

import jax
import jax.numpy as jnp
from jax import lax
from jax.experimental import pallas as pl
from jax.experimental.pallas import tpu as pltpu
from jax.sharding import PartitionSpec as P

D = 8192
RANK = 512
BLOCK = 128
ROWS_D = D // BLOCK
ROWS_K = RANK // BLOCK
NBLK = ROWS_D * ROWS_K
EPS = 1e-05
CHUNK = 1024
BLOCKS = CHUNK // BLOCK
NT = (((1,), (1,)), ((), ()))
NN = (((1,), (0,)), ((), ()))
TN = (((0,), (0,)), ((), ()))
PAIR = [(0, 1), (1, 0), (2, 3), (3, 2)]
UP = [(0, 3), (1, 2)]
DOWN = [(3, 0), (2, 1)]
RING = 4
Y = 2
Z = 8
NEAR = ((0, 3, 1, 2), (0, 1, 3, 2))
FAR = ((0, 3), (1, 2))
CORES = [(i, i ^ 1) for i in range(Z * RING)]


def dot(left, right, dims):
    return lax.dot_general(left, right, dims, preferred_element_type=jnp.float32)


class Weights:
    def __init__(self, swap_ref, where_ref, source, held, sems, wanted):
        self.where_ref = where_ref
        self.swap = swap_ref[0]
        self.held = held
        self.order = wanted
        owners = source.shape[0]
        self.copies = {}
        for i, (layer, matrix) in enumerate(wanted):
            copy = pltpu.make_async_copy(source.at[:, layer ^ self.swap, matrix], held.at[i, pl.ds(0, owners)], sems.at[i])
            copy.start()
            self.copies[layer, matrix] = copy
        for i in range(len(wanted)):
            held[i, owners, 0] = jnp.zeros(held.shape[3:], held.dtype)

    def wait(self, layer, matrix):
        copy = self.copies.pop((layer, matrix), None)
        if copy is not None:
            copy.wait()

    def block(self, layer, matrix, number):
        code = self.where_ref[((layer ^ self.swap) * 2 + matrix) * NBLK + number]
        return self.held[self.order.index((layer, matrix)), code >> 3, code & 7]

    def rows_in(self, layer, chunk):
        rows = range(chunk * BLOCKS, (chunk + 1) * BLOCKS)
        return jnp.concatenate(
            [
                jnp.concatenate([self.block(layer, 0, row * ROWS_K + col) for col in range(ROWS_K)], axis=1)
                for row in rows
            ],
            axis=0,
        )

    def columns_out(self, layer, chunk):
        cols = range(chunk * BLOCKS, (chunk + 1) * BLOCKS)
        return jnp.concatenate(
            [
                jnp.concatenate([self.block(layer, 1, row * ROWS_D + col) for col in cols], axis=1)
                for row in range(ROWS_K)
            ],
            axis=0,
        )


def chunks():
    return [(chunk, slice(chunk * CHUNK, (chunk + 1) * CHUNK)) for chunk in range(D // CHUNK)]


def forward_down(weights, layer, hidden_ref, normed_ref):
    total = 0.0
    for _, cols in chunks():
        wide = hidden_ref[:, cols].astype(jnp.float32)
        total = total + jnp.sum(wide * wide, axis=-1, keepdims=True)
    inverse = 1.0 / jnp.sqrt(total / D + EPS)
    for _, cols in chunks():
        normed_ref[:, cols] = (hidden_ref[:, cols].astype(jnp.float32) * inverse).astype(jnp.bfloat16)
    weights.wait(layer, 0)
    pre = 0.0
    for chunk, cols in chunks():
        pre = pre + dot(normed_ref[:, cols], weights.rows_in(layer, chunk), NN)
    return pre, inverse


def forward_up(weights, layer, hidden_ref, act, next_ref):
    weights.wait(layer, 1)
    for chunk, cols in chunks():
        moved = dot(act, weights.columns_out(layer, chunk), NN)
        next_ref[:, cols] = (hidden_ref[:, cols].astype(jnp.float32) + moved).astype(jnp.bfloat16)


def backward(weights, layer, hidden_ref, upstream_ref, pre, inverse, earlier_ref):
    weights.wait(layer, 1)
    dact = 0.0
    for chunk, cols in chunks():
        dact = dact + dot(upstream_ref[:, cols], weights.columns_out(layer, chunk), NT)
    sig = jax.nn.sigmoid(pre)
    dpre = (dact * sig * (1.0 + pre * (1.0 - sig))).astype(jnp.bfloat16)
    if earlier_ref is not None:
        mean = jnp.sum(dpre.astype(jnp.float32) * pre, axis=-1, keepdims=True) / D
        pull = mean * inverse * inverse
        weights.wait(layer, 0)
        for chunk, cols in chunks():
            dnorm = dot(dpre, weights.rows_in(layer, chunk), NT)
            hidden = hidden_ref[:, cols].astype(jnp.float32)
            earlier_ref[:, cols] = (
                upstream_ref[:, cols].astype(jnp.float32) + dnorm * inverse - hidden * pull
            ).astype(jnp.bfloat16)
    return dpre


def silu(pre):
    return (pre * jax.nn.sigmoid(pre)).astype(jnp.bfloat16)


def forward_kernel(swap_ref, where_ref, first_ref, source, last_ref, second_ref, normed_ref, held, sems):
    weights = Weights(swap_ref, where_ref, source, held, sems, [(0, 0), (0, 1), (1, 0), (1, 1)])
    pre, _ = forward_down(weights, 0, first_ref, normed_ref)
    forward_up(weights, 0, first_ref, silu(pre), second_ref)
    pre, _ = forward_down(weights, 1, second_ref, normed_ref)
    forward_up(weights, 1, second_ref, silu(pre), last_ref)


class Choice:
    def __init__(self, arrived, arrived_ref, here_ref, out_ref, sem):
        self.arrived = arrived
        self.copy = pltpu.make_async_copy(arrived_ref, out_ref, sem)

        @pl.when(arrived)
        def _():
            self.copy.start()

        @pl.when(jnp.logical_not(arrived))
        def _():
            out_ref[...] = here_ref[...]

    def wait(self):
        @pl.when(self.arrived)
        def _():
            self.copy.wait()


def turn_kernel(
    swap_ref, where_ref, tokens_ref, arrived_ref, grad_ref, source, second_ref, pre_ref, inverse_ref, normed_own_ref, normed_other_ref, act_own_ref, act_other_ref, earlier_ref, first_ref, middle_ref, normed_ref, act_ref, held, sems
):
    choice = Choice(swap_ref[1] > 0, arrived_ref, tokens_ref, first_ref, sems.at[4])
    weights = Weights(swap_ref, where_ref, source, held, sems, [(0, 0), (0, 1), (1, 0), (1, 1)])
    choice.wait()
    for layer, hidden_ref in enumerate((first_ref, second_ref)):
        place = layer ^ swap_ref[0]
        pre, inverse = forward_down(weights, layer, hidden_ref, normed_ref.at[place])
        act = silu(pre)
        pre_ref[layer] = pre
        inverse_ref[layer] = jnp.broadcast_to(inverse, inverse_ref.shape[1:])
        act_ref[place] = act
        if layer == 0:
            forward_up(weights, 0, first_ref, act, second_ref)
    act_own_ref[...], act_other_ref[...] = act_ref[0], act_ref[1]
    for _, cols in chunks():
        normed_own_ref[:, cols] = normed_ref[0, :, cols]
        normed_other_ref[:, cols] = normed_ref[1, :, cols]
    backward(weights, 1, second_ref, grad_ref, pre_ref[1], inverse_ref[1][:, :1], middle_ref)
    backward(weights, 0, first_ref, middle_ref, pre_ref[0], inverse_ref[0][:, :1], earlier_ref)


def high_kernel(
    swap_ref, where_ref, hidden_ref, grad_ref, arrived_ref, pre_ref, inverse_ref, source, dpre_ref, middle_ref, own_ref, sent_ref, upstream_ref, held, sems
):
    choice = Choice(swap_ref[1] == 0, arrived_ref, grad_ref, upstream_ref, sems.at[2])
    weights = Weights(swap_ref, where_ref, source, held, sems, [(1, 1), (1, 0)])
    even = swap_ref[0] == 0
    choice.wait()
    dpre_ref[...] = backward(weights, 1, hidden_ref, upstream_ref, pre_ref[1], inverse_ref[1][:, :1], middle_ref)
    for _, cols in chunks():
        upper, lower = upstream_ref[:, cols], middle_ref[:, cols]
        own_ref[:, cols] = lax.select(even, lower, upper)
        sent_ref[:, cols] = lax.select(even, upper, lower)


def low_kernel(swap_ref, where_ref, middle_ref, high_ref, pre_ref, source, own_ref, sent_ref, held, sems):
    weights = Weights(swap_ref, where_ref, source, held, sems, [(0, 1)])
    even = swap_ref[0] == 0
    low = backward(weights, 0, None, middle_ref, pre_ref[0], None, None)
    high = high_ref[...]
    own_ref[...] = lax.select(even, low, high)
    sent_ref[...] = lax.select(even, high, low)


def by_step(values):
    step = pl.program_id(0)
    result = values[0]
    for i, value in enumerate(values[1:], 1):
        result = lax.select(step == i, jnp.int32(value), jnp.int32(result))
    return result


def pick(spots_ref, places_ref, strides, dense, keep_ref, send_ref):
    slots = keep_ref.shape[2]
    for which in range(2):
        near = spots_ref[0] ^ by_step([group[step * 2 + which] for group in NEAR for step in range(2)])
        for other in range(2):
            far = spots_ref[1] ^ by_step([group[other] for group in FAR for _ in range(2)])
            for half, out_ref in enumerate((keep_ref, send_ref)):
                owner = near * strides[0] + far * strides[1] + (spots_ref[2] ^ half)
                for slot in range(slots):
                    out_ref[0, which * 2 + other, slot] = dense[places_ref[owner * slots + slot]]


def gradient_in_kernel(spots_ref, places_ref, own_ref, other_ref, dpre_own_ref, dpre_other_ref, keep_ref, send_ref, dense):
    @pl.when(pl.program_id(0) == 0)
    def _():
        dense[NBLK] = jnp.zeros((BLOCK, BLOCK), jnp.bfloat16)
        dpre = jnp.concatenate([dpre_own_ref[...], dpre_other_ref[...]], axis=0)
        for chunk, cols in chunks():
            normed = jnp.concatenate([own_ref[:, cols], other_ref[:, cols]], axis=0)
            part = dot(normed, dpre, TN).astype(jnp.bfloat16)
            for row in range(BLOCKS):
                for col in range(ROWS_K):
                    dense[(chunk * BLOCKS + row) * ROWS_K + col] = part[
                        row * BLOCK : (row + 1) * BLOCK, col * BLOCK : (col + 1) * BLOCK
                    ]

    pick(spots_ref, places_ref, (Y, Z), dense, keep_ref, send_ref)


def gradient_out_kernel(
    spots_ref, places_ref, act_own_ref, act_other_ref, own_ref, other_ref, keep_ref, send_ref, dense, turned
):
    @pl.when(pl.program_id(0) == 0)
    def _():
        dense[NBLK] = jnp.zeros((BLOCK, BLOCK), jnp.bfloat16)
        act = jnp.concatenate([act_own_ref[...], act_other_ref[...]], axis=0)
        turned[...] = act.astype(jnp.float32).T.astype(jnp.bfloat16)
        for chunk, cols in chunks():
            upstream = jnp.concatenate([own_ref[:, cols], other_ref[:, cols]], axis=0)
            part = dot(turned[...], upstream, NN).astype(jnp.bfloat16)
            for row in range(ROWS_K):
                for col in range(BLOCKS):
                    dense[row * ROWS_D + chunk * BLOCKS + col] = part[
                        row * BLOCK : (row + 1) * BLOCK, col * BLOCK : (col + 1) * BLOCK
                    ]

    pick(spots_ref, places_ref, (Z, Y), dense, keep_ref, send_ref)


def whole(*shape):
    return pl.BlockSpec(shape, lambda step, *_: (0,) * len(shape))


def params(flops, moved):
    return dict(
        compiler_params=pltpu.CompilerParams(
            dimension_semantics=("arbitrary",), vmem_limit_bytes=56 * 1024 * 1024
        ),
        cost_estimate=pl.CostEstimate(flops=flops, bytes_accessed=moved, transcendentals=0),
    )


def across(array, stride, flip):
    if flip == 0:
        return array
    devices = range(lax.axis_size("dp"))
    return lax.ppermute(array, "dp", [(i, i + ((i // stride % RING ^ flip) - i // stride % RING) * stride) for i in devices])


def rounded_sum(*terms):
    return sum(term.astype(jnp.float32) for term in terms).astype(jnp.bfloat16)


def swapped(array):
    return lax.ppermute(array, "section", PAIR)


def per_device(tokens, blocks_in, blocks_out, pos_in, pos_out, cotangent):
    here = lax.axis_index("section")
    owners = lax.axis_size("dp")
    slots = blocks_in.shape[1]
    rows = tokens.shape[0] // 2
    odd = here % 2
    swap = jnp.stack([odd, here // 2]).astype(jnp.int32)
    half = jnp.where((here == 1) | (here == 2), rows, 0)

    both = jnp.stack([blocks_in[0], blocks_out[0], swapped(blocks_in[0]), swapped(blocks_out[0])])
    weights = lax.all_gather(both, "dp", axis=0).reshape(owners, 2, 2, slots, BLOCK, BLOCK)
    own_places = jnp.stack([pos_in[0], pos_out[0]])
    places = lax.all_gather(jnp.stack([own_places, swapped(own_places)]), "dp", axis=0).transpose(1, 2, 0, 3)
    codes = jnp.arange(owners, dtype=jnp.int32)[:, None] * 8 + jnp.arange(slots, dtype=jnp.int32)
    named = places[..., None] == jnp.arange(NBLK, dtype=jnp.int32)
    where = jnp.max(jnp.where(named, codes[..., None], -1), axis=(2, 3)).reshape(-1)
    where = jnp.where(where < 0, owners * 8, where)
    places_in, places_out = places[0, 0].reshape(-1), places[0, 1].reshape(-1)
    me = lax.axis_index("dp")
    spot_z, spot_y, spot_core = me // Z, me // Y % RING, me % Y
    spots_in = jnp.stack([spot_y, spot_z, spot_core]).astype(jnp.int32)
    spots_out = jnp.stack([spot_z, spot_y, spot_core]).astype(jnp.int32)
    where, places_in, places_out, spots_in, spots_out = lax.optimization_barrier(
        (where, places_in, places_out, spots_in, spots_out)
    )

    first_tokens = lax.dynamic_slice_in_dim(tokens, half, rows, 0)
    last_grads = lax.dynamic_slice_in_dim(cotangent, half, rows, 0)

    def shape(*dims, dtype=jnp.bfloat16):
        return jax.ShapeDtypeStruct(dims, dtype)

    moved = weights.size * 2
    work = 2 * rows * D * RANK
    anywhere = pl.BlockSpec(memory_space=pl.ANY)

    def held(count):
        return [
            pltpu.VMEM((count, owners + 1, slots, BLOCK, BLOCK), jnp.bfloat16),
            pltpu.SemaphoreType.DMA((count + 1,)),
        ]

    forward = pl.pallas_call(
        forward_kernel,
        out_shape=shape(rows, D),
        grid_spec=pltpu.PrefetchScalarGridSpec(
            num_scalar_prefetch=2,
            grid=(1,),
            in_specs=[whole(rows, D), anywhere],
            out_specs=whole(rows, D),
            scratch_shapes=[pltpu.VMEM((rows, D), jnp.bfloat16), pltpu.VMEM((rows, D), jnp.bfloat16)] + held(4),
        ),
        name="forward_layers",
        **params(4 * work, moved),
    )
    turn = pl.pallas_call(
        turn_kernel,
        out_shape=(
            shape(rows, D),
            shape(2, rows, RANK, dtype=jnp.float32),
            shape(2, rows, BLOCK, dtype=jnp.float32),
            shape(rows, D),
            shape(rows, D),
            shape(rows, RANK),
            shape(rows, RANK),
            shape(rows, D),
        ),
        grid_spec=pltpu.PrefetchScalarGridSpec(
            num_scalar_prefetch=2,
            grid=(1,),
            in_specs=[whole(rows, D), anywhere, whole(rows, D), anywhere],
            out_specs=[
                whole(rows, D),
                whole(2, rows, RANK),
                whole(2, rows, BLOCK),
                whole(rows, D),
                whole(rows, D),
                whole(rows, RANK),
                whole(rows, RANK),
                whole(rows, D),
            ],
            scratch_shapes=[pltpu.VMEM((rows, D), jnp.bfloat16)] * 2
            + [pltpu.VMEM((2, rows, D), jnp.bfloat16), pltpu.VMEM((2, rows, RANK), jnp.bfloat16)]
            + held(4),
        ),
        name="turn_layers",
        **params(7 * work, moved),
    )

    high = pl.pallas_call(
        high_kernel,
        out_shape=(shape(rows, RANK),) + (shape(rows, D),) * 3,
        grid_spec=pltpu.PrefetchScalarGridSpec(
            num_scalar_prefetch=2,
            grid=(1,),
            in_specs=[whole(rows, D)] * 2 + [anywhere, whole(2, rows, RANK), whole(2, rows, BLOCK), anywhere],
            out_specs=[whole(rows, RANK)] + [whole(rows, D)] * 3,
            scratch_shapes=[pltpu.VMEM((rows, D), jnp.bfloat16)] + held(2),
        ),
        name="backward_high",
        **params(2 * work, moved // 2),
    )
    low = pl.pallas_call(
        low_kernel,
        out_shape=(shape(rows, RANK), shape(rows, RANK)),
        grid_spec=pltpu.PrefetchScalarGridSpec(
            num_scalar_prefetch=2,
            grid=(1,),
            in_specs=[whole(rows, D), whole(rows, RANK), whole(2, rows, RANK), anywhere],
            out_specs=[whole(rows, RANK)] * 2,
            scratch_shapes=held(1),
        ),
        name="backward_low",
        **params(work, moved),
    )

    halves = shape(RING, RING, slots, BLOCK, BLOCK)
    half_spec = pl.BlockSpec((1, RING, slots, BLOCK, BLOCK), lambda step, *_: (step, 0, 0, 0, 0))
    dense = pltpu.VMEM((NBLK + 1, BLOCK, BLOCK), jnp.bfloat16)

    def gradient(kernel, name, in_specs, scratch):
        return pl.pallas_call(
            kernel,
            out_shape=(halves, halves),
            grid_spec=pltpu.PrefetchScalarGridSpec(
                num_scalar_prefetch=2,
                grid=(RING,),
                in_specs=in_specs,
                out_specs=(half_spec, half_spec),
                scratch_shapes=[dense] + scratch,
            ),
            name=name,
            **params(2 * work, 3 * moved),
        )

    gradient_in = gradient(
        gradient_in_kernel, "gradient_in", [whole(rows, D)] * 2 + [whole(rows, RANK)] * 2, []
    )
    gradient_out = gradient(
        gradient_out_kernel,
        "gradient_out",
        [whole(rows, RANK)] * 2 + [whole(rows, D)] * 2,
        [pltpu.VMEM((RANK, 2 * rows), jnp.bfloat16)],
    )
    def core_sums(keep, send):
        arrived = lax.ppermute(send, "dp", CORES)
        return [rounded_sum(keep[i], arrived[i]) for i in range(RING)]

    def scattered(pieces, near, far):
        sums = []
        for kept, sent, (_, second, first, _) in zip(pieces[::2], pieces[1::2], NEAR):
            arrived = across(sent, near, first)
            mine = rounded_sum(kept[:2], arrived[:2])
            arrived = across(rounded_sum(kept[2:], arrived[2:]), near, second)
            sums += [rounded_sum(mine[i], arrived[i]) for i in range(2)]
        return rounded_sum(*[across(term, far, step) for term, step in zip(sums, FAR[0] + FAR[1])])[None]

    arrived = lax.ppermute(forward(swap, where, first_tokens, weights), "section", UP)
    second, pre, inverse, normed_own, normed_sent, act_own, act_sent, leaving = turn(swap, where, first_tokens, arrived, last_grads, weights)
    arrived = lax.ppermute(leaving, "section", DOWN)
    normed_sent, act_other = lax.optimization_barrier((normed_sent, swapped(act_sent)))
    arrived, normed_other = lax.optimization_barrier((arrived, swapped(normed_sent)))

    dpre_high, middle, grads_own, sent = high(swap, where, second, last_grads, arrived, pre, inverse, weights)
    grads_other = swapped(sent)
    dpre_own, dpre_sent = low(swap, where, middle, dpre_high, pre, weights)
    grads_other, dpre_other = lax.optimization_barrier((grads_other, swapped(dpre_sent)))

    halves_in = gradient_in(spots_in, places_in, normed_own, normed_other, dpre_own, dpre_other)
    halves_out = gradient_out(spots_out, places_out, act_own, act_other, grads_own, grads_other)
    pieces_in, pieces_out = core_sums(*halves_in), core_sums(*halves_out)
    sums_in = scattered(pieces_in, Y, Z)
    sums_out = scattered(pieces_out, Z, Y)
    return (sums_in, sums_out)


def solution(mesh):
    in_specs = (
        P("dp", None),
        P("section", "dp", None, None),
        P("section", "dp", None, None),
        P("section", "dp"),
        P("section", "dp"),
        P("dp", None),
    )
    out_specs = (P("section", "dp", None, None), P("section", "dp", None, None))
    return jax.shard_map(
        per_device, mesh=mesh, in_specs=in_specs, out_specs=out_specs, check_vma=False
    )
```
